256 devices in a mesh: blk: 32 (over x, z_lo, core), dom: 8 (over y, z_hi).
Axes of the slice: x: 4, y: 4, z: 8 (z_hi: 2, z_lo: 4; z = z_hi * 4 + z_lo), core: 2. Of those that a mesh axis runs over, the one named last changes fastest.
Arguments:
- particles: bfloat16 [1024, 128, 128], P(('blk', 'dom')), may hold values from -8 to 8
- defocus: float32 [1024], P(('blk', 'dom')), may hold values from 290 to 3010
- noise_weight: float32 [128, 64], replicated, may hold values from 0.005 to 0.05
- projections: bfloat16 [8, 32, 128, 128], P(None, 'blk'), may hold values from -6 to 6
- row_slab: int32 [1024, 128, 1], P(('blk', 'dom')), may hold values from 0 to 31, as said below
- row_slot: int32 [1024, 128], P(('blk', 'dom')), may hold values from 0 to 511, as said below
- interp: float32 [1024, 128], P(('blk', 'dom')), may hold values from 0.25 to 1
Outputs:
- volume: float32 [8, 16384, 128], P(None, ('blk', 'dom'))
- class_weight: float32 [1024, 8], P(('blk', 'dom'))
The draws below stay inside these ranges and needn't reach their ends.
Inputs may be any that keep to these rules, and one draw needn't show every extreme that they name: `row_slab`: the rows of one device's particles (aligned blocks of 512 rows) put at most 32 rows into one slab, and exactly 32 into some slab. Piece p of a slab holds the rows with row_slot from p * 64 to (p + 1) * 64 - 1. The rows of one device's particles put at most 4 rows into one piece of one slab, and exactly 4 into some piece.
All inputs are finite; a program needn't handle non-finite values.
Results may differ from the reference program's by a relative error of at most 0.033.
Values may be sent and summed in bfloat16 or wider, within the bound.
A program may use at most 128 MiB of HBM per device.

```python
import math
import jax
import jax.numpy as jnp
from jax import lax

IMG = 128
CLASSES = 8
SHIFTS = 9
NP_DEV = 4
HALF = 64
NORI = 32
PARTICLES = 1024
VOL_ROWS = 16384
SLAB_ROWS = 512
N_BLK = 32
N_DOM = 8


def shared_fields(key):
    proj_key = jax.random.fold_in(key, 101)
    focus_key = jax.random.fold_in(key, 202)
    projections = jnp.clip(jax.random.normal(proj_key, (CLASSES, NORI, IMG, IMG), jnp.float32), -6.0, 6.0)
    defocus = jnp.exp(jax.random.uniform(focus_key, (PARTICLES,), jnp.float32, math.log(300.0), math.log(3000.0)))
    return (projections, defocus)


def shared_routes(key):
    route_key = jax.random.fold_in(key, 303)
    device_count = N_BLK * N_DOM
    rows_device = NP_DEV * IMG
    bucket_count = N_BLK * N_DOM
    base_load = rows_device // bucket_count
    order_key, hot_key, shuffle_key, within_key = jax.random.split(route_key, 4)
    order_keys = jax.random.split(order_key, device_count)
    shuffle_keys = jax.random.split(shuffle_key, device_count)
    hot_counts = jax.random.randint(hot_key, (device_count,), 1, max(1, N_BLK // 4) + 1)

    def one_device(order_seed, shuffle_seed, hot_count):
        slab_order = jax.random.permutation(order_seed, N_BLK)
        slab_rank = jnp.zeros((N_BLK,), jnp.int32).at[slab_order].set(jnp.arange(N_BLK, dtype=jnp.int32))
        multiple = jnp.where(slab_rank < hot_count, 2, jnp.where(slab_rank < 2 * hot_count, 0, 1)).astype(jnp.int32)
        loads = jnp.repeat(multiple * base_load, N_DOM)
        ends = jnp.cumsum(loads)
        positions = jnp.arange(rows_device, dtype=jnp.int32)
        bucket = jnp.searchsorted(ends, positions, side='right').astype(jnp.int32)
        return jax.random.permutation(shuffle_seed, bucket)
    buckets = jax.vmap(one_device)(order_keys, shuffle_keys, hot_counts).reshape(PARTICLES, IMG)
    slab_ids = buckets // N_DOM
    piece_ids = buckets % N_DOM
    piece_rows = SLAB_ROWS // N_DOM
    slot_ids = piece_ids * piece_rows + jax.random.randint(within_key, (PARTICLES, IMG), 0, piece_rows)
    return (slab_ids.astype(jnp.int32), slot_ids.astype(jnp.int32))


def draw_row_slab(key, part):
    slab_ids, slot_ids = shared_routes(key)
    return slab_ids[:, :, None]


def draw_row_slot(key, part):
    slab_ids, slot_ids = shared_routes(key)
    return slot_ids


def draw_projections(key, part):
    projections, defocus = shared_fields(key)
    return projections.astype(jnp.bfloat16)


def draw_defocus(key, part):
    projections, defocus = shared_fields(key)
    return defocus


def draw_particles(key, part):
    key = jax.random.fold_in(key, 3)
    noise_key = jax.random.fold_in(key, 0)
    values = jax.random.normal(noise_key, (PARTICLES, IMG, IMG), jnp.float32)
    return jnp.clip(values, -8.0, 8.0).astype(jnp.bfloat16)


def steps_of(own_key, extent, pieces, low, largest):
    loudness, own = 1.0, jax.random.fold_in(own_key, 6)
    for position, parts in pieces:
        draws = jnp.exp(jax.random.uniform(jax.random.fold_in(own, position), (parts,), jnp.float32, low / len(pieces), largest / len(pieces)))
        loudness = loudness * jnp.repeat(draws, extent[position] // parts).reshape([-1 if axis == position else 1 for axis in range(len(extent))])
    return loudness


def setup_inputs(seed: int = 0) -> dict:
    streams_of = jax.random.split(jax.random.key(seed), 8)
    return {
        "particles": draw_particles(jax.random.fold_in(streams_of[7], 71), 0),
        "defocus": draw_defocus(jax.random.fold_in(streams_of[7], 71), 0),
        "noise_weight": jnp.clip(jnp.exp(jax.random.uniform(streams_of[2], (IMG, HALF), jnp.float32, math.log(0.005), math.log(0.05))), 0.005, 0.05),
        "projections": draw_projections(jax.random.fold_in(streams_of[7], 71), 0),
        "row_slab": draw_row_slab(jax.random.fold_in(streams_of[7], 71), 0),
        "row_slot": draw_row_slot(jax.random.fold_in(streams_of[7], 71), 0),
        "interp": jnp.clip(0.25 + 0.75 * jax.random.uniform(streams_of[6], (PARTICLES, IMG), jnp.float32) ** steps_of(streams_of[6], (PARTICLES, IMG), ((0, 256),), -0.2, 0.2), 0.25, 1.0),
    }


def spectrum(image_side):
    freq_index = jnp.arange(image_side)
    half_width = image_side // 2
    row_freq = jnp.where(freq_index < half_width, freq_index, freq_index - image_side).astype(jnp.float32)
    col_freq = (freq_index % half_width).astype(jnp.float32)
    return row_freq[:, None], col_freq[None, :]


def transfer_curve(defocus, image_side):
    row_freq, col_freq = spectrum(image_side)
    radius = (col_freq * col_freq + row_freq * row_freq) / float(image_side * image_side)
    return -jnp.sin(defocus[:, None, None] * radius[None] + 0.1)


def phase_tables(image_side, shift_count):
    row_freq, col_freq = spectrum(image_side)
    offsets = jnp.arange(shift_count)
    shift_x = (offsets % 3 - 1).astype(jnp.float32)[:, None, None]
    shift_y = (offsets // 3 - 1).astype(jnp.float32)[:, None, None]
    phase_angle = (2.0 * math.pi / image_side) * (col_freq[None] * shift_x + row_freq[None] * shift_y)
    return jnp.cos(phase_angle), jnp.sin(phase_angle)


def turn(values, cosine, sine_table):
    half_width = values.shape[-1] // 2
    swapped = jnp.concatenate([-values[..., half_width:], values[..., :half_width]], axis=-1)
    return (values * cosine + swapped * sine_table).astype(jnp.bfloat16)


def reference(particles, defocus, noise_weight, projections, row_slab, row_slot, interp):
    image_side = IMG
    ctf_curve = transfer_curve(defocus, image_side)
    noise_full = jnp.concatenate([noise_weight, noise_weight], axis=1)
    image_data = particles.astype(jnp.float32)
    weighted = (ctf_curve * noise_full * image_data).astype(jnp.bfloat16)
    norm_weight = (ctf_curve * ctf_curve * noise_full).astype(jnp.bfloat16).reshape(PARTICLES, -1)
    inserted = (ctf_curve * image_data).astype(jnp.bfloat16)
    cosines, sine_tables = phase_tables(image_side, SHIFTS)
    values = projections.astype(jnp.float32)
    power_table = (values * values).astype(jnp.bfloat16).reshape(CLASSES * NORI, -1)
    proj_flat = values.reshape(CLASSES * NORI, -1)
    weighted_wide = weighted.astype(jnp.float32)
    penalty = 0.5 * jnp.dot(norm_weight.astype(jnp.float32), power_table.astype(jnp.float32).T, precision=lax.Precision.HIGHEST)
    columns = []
    for shift_index in range(SHIFTS):
        turned = turn(weighted_wide, cosines[shift_index], -sine_tables[shift_index]).reshape(PARTICLES, -1)
        columns.append(jnp.dot(turned.astype(jnp.float32), proj_flat.T, precision=lax.Precision.HIGHEST) - penalty)
    scores = jnp.stack(columns, axis=1)
    flat_scores = scores.reshape(PARTICLES, -1)
    row_top = jnp.max(flat_scores, axis=1, keepdims=True)
    exp_scores = jnp.exp(flat_scores - row_top)
    posterior = exp_scores / jnp.sum(exp_scores, axis=1, keepdims=True)
    class_weight = jnp.sum(posterior.reshape(PARTICLES, SHIFTS, CLASSES, NORI), axis=(1, 3))
    coefficient = interp[:, :, None] * class_weight[:, None, :]
    target = (row_slab[:, :, 0].astype(jnp.int32) * SLAB_ROWS + row_slot.astype(jnp.int32)).astype(jnp.int32)
    group_size = NP_DEV * N_DOM
    blocks = PARTICLES // group_size

    def insert(running, block_index):
        first_row = (block_index * group_size).astype(jnp.int32)
        row_data = lax.dynamic_slice_in_dim(inserted, first_row, group_size, 0).astype(jnp.float32)
        coef_data = lax.dynamic_slice_in_dim(coefficient, first_row, group_size, 0)
        row_target = lax.dynamic_slice_in_dim(target, first_row, group_size, 0).reshape(-1)
        rounded = (coef_data[:, :, :, None] * row_data[:, :, None, :]).astype(jnp.bfloat16)
        rounded = lax.optimization_barrier(rounded)
        product = rounded.astype(jnp.float32).reshape(group_size * image_side, CLASSES * image_side)
        return running.at[row_target].add(product), None

    volume, _ = lax.scan(insert, jnp.zeros((VOL_ROWS, CLASSES * image_side), jnp.float32), jnp.arange(blocks).astype(jnp.int32))
    volume = volume.reshape(VOL_ROWS, CLASSES, image_side).transpose(1, 0, 2)
    return volume, class_weight
```

```python
import jax
import jax.numpy as jnp
from jax import lax
from jax.experimental import pallas as pl
from jax.experimental.pallas import tpu as pltpu
from jax.sharding import PartitionSpec as P

F32, BF16 = jnp.float32, jnp.bfloat16
MESH = pl.DeviceIdType.MESH
PI = 3.141592653589793
SIN_COEF = (
    0.9999999992267364, -0.16666665898756483, 0.008333320916259667, -0.00019840515744570079,
    2.7535452887970435e-06, -2.47248903062851e-08, 1.3598699876951359e-10,
)
SIN2_COEF = (
    0.9999999902438815, -0.3333330511544617, 0.044443119935340766, -0.00317232337316227,
    0.00013931019440764148, -3.6240280738953943e-06,
)


def reduced(angle, period, high, mid):
    turns = jnp.floor(angle * (1.0 / period) + 0.5)
    return ((angle - turns * high) - turns * mid) - turns * (period - high - mid)


def horner(coef, y):
    total = jnp.full_like(y, coef[-1])
    for c in coef[-2::-1]:
        total = total * y + c
    return total


def sine(angle):
    r = reduced(angle, 2 * PI, 6.28125, 8117 / 2**22)
    return r * horner(SIN_COEF, r * r)


def sine_squared(angle):
    r = reduced(angle, PI, 3.140625, 8117 / 2**23)
    y = r * r
    return y * horner(SIN2_COEF, y)


def iota(shape, axis):
    return lax.broadcasted_iota(jnp.int32, shape, axis)


def dot(a, b):
    return jnp.dot(a, b, preferred_element_type=F32)


def dot_nt(a, b):
    return lax.dot_general(a, b, (((1,), (1,)), ((), ())), preferred_element_type=F32)


def split_dot(values, indicator):
    high = values.astype(BF16)
    low = (values - high.astype(F32)).astype(BF16)
    return dot(high, indicator) + dot(low, indicator)


def kernel(
    part_ref, focus_ref, noise_ref, proj_ref, slab_ref, slot_ref, interp_ref,
    vol_ref, cw_ref,
    wide_p, wide_x, noise_full, cols, weight_in, proj_in, focus_in, rows_ins,
    left_op, right_op, score, turn_tab, hop1_out, hop1_in, hop2_out, hop2_in, stat, cwt, cw_flat, coef_tab,
    w_send, w_recv, p_send, p_recv, f_send, f_recv, h1_send, h1_recv, h2_send, h2_recv,
    s_send, s_recv, c_send, c_recv,
):
    blk, dom = lax.axis_index("blk"), lax.axis_index("dom")
    x, a = blk // 8, blk % 8
    z, core = a // 2, a % 2
    g = x * 8 + dom

    def copy(src, dst, send, recv, to_blk, to_dom):
        return pltpu.make_async_remote_copy(
            src_ref=src, dst_ref=dst, send_sem=send, recv_sem=recv,
            device_id=(to_blk, to_dom), device_id_type=MESH,
        )

    def a_peer(i):
        return (a + i) % 8

    def g_peer(i):
        return (g + i) % 32

    barrier = pltpu.get_barrier_semaphore()

    def greet_a(i, _):
        pl.semaphore_signal(barrier, inc=1, device_id=(x * 8 + a_peer(i), dom), device_id_type=MESH)
        return 0

    def greet_g(i, _):
        to = g_peer(i)
        pl.semaphore_signal(barrier, inc=1, device_id=((to // 8) * 8 + a, to % 8), device_id_type=MESH)
        return 0

    lax.fori_loop(1, 8, greet_a, 0)
    lax.fori_loop(1, 32, greet_g, 0)

    wide_x[...] = proj_ref[...].astype(F32)

    def order_proj(q, _):
        tile = wide_x[pl.ds(q, 16, stride=64), :].astype(BF16)
        proj_in[x, pl.ds(pl.multiple_of(q * 16, 16), 16), :] = tile
        return 0

    lax.fori_loop(0, 64, order_proj, 0, unroll=4)

    pl.semaphore_wait(barrier, 38)

    right, left = ((x + 1) % 4) * 8 + a, ((x + 3) % 4) * 8 + a
    top, low = pl.ds(0, 512), pl.ds(512, 512)

    def p_copy(k, block, half, to):
        return copy(proj_in.at[block, half], proj_in.at[block, half], p_send.at[k], p_recv.at[k], to, dom)

    p_copy(0, x, top, right).start()
    p_copy(2, x, low, left).start()
    p_copy(1, x, low, right).start()
    p_copy(3, x, top, left).start()

    focus_in[a] = focus_ref[...]

    def f_copy(i):
        return copy(focus_in.at[a], focus_in.at[a], f_send.at[i], f_recv.at[i], x * 8 + a_peer(i), dom)

    lax.fori_loop(1, 8, lambda i, _: (f_copy(i).start(), 0)[1], 0)

    noise_full[...] = jnp.concatenate([noise_ref[...], noise_ref[...]], axis=1)
    interp = interp_ref[...]
    for p in range(4):
        cols[p * 128:(p + 1) * 128, :] = jnp.broadcast_to(interp[p:p + 1, :], (128, 128)).T
    wide_p[...] = part_ref[...].astype(F32)
    lane8 = iota((8, 128), 1)
    kx = (lane8 % 64).astype(F32)
    kx2 = kx * kx
    odd8 = (iota((8, 128), 0) % 2) == 1
    half8 = lane8 < 64
    focus = focus_ref[...]

    def weigh(q2, _):
        tiles = []
        for h in range(2):
            q = q2 * 2 + h
            rows = pl.ds(q, 8, stride=64)
            image = wide_p[rows, :]
            ky = jnp.where(odd8, q - 64, q).astype(F32)
            radius = (kx2 + ky * ky) * (1.0 / 16384.0)
            signal = -sine(focus * radius + 0.1) * image
            noise = jnp.where(odd8, noise_full[pl.ds(q + 64, 1), :], noise_full[pl.ds(q, 1), :])
            tiles.append(signal * noise)
            rows_ins[rows, :] = signal * cols[rows, :]
        weight_in[a, pl.ds(pl.multiple_of(q2 * 16, 16), 16), :] = jnp.concatenate(tiles, axis=0).astype(BF16)
        return 0

    lax.fori_loop(0, 32, weigh, 0, unroll=2)

    def w_copy(k, block, to):
        return copy(weight_in.at[block], weight_in.at[block], w_send.at[k], w_recv.at[k], x * 8 + to, dom)

    for i in range(1, 4):
        w_copy(i, a, ((z + i) % 4) * 2 + core).start()
    w_copy(0, a, z * 2 + 1 - core).start()

    slab, slot = slab_ref[...], slot_ref[...]
    piece = slot // 64
    bucket = (slab * 8 + piece).astype(F32)
    earlier = iota((128, 128), 0) < iota((128, 128), 1)
    ranks = []
    across = [jnp.broadcast_to(bucket[p:p + 1, :], (128, 128)) for p in range(4)]
    down = [b.T for b in across]
    for p in range(4):
        rank = jnp.zeros((1, 128), F32)
        for p2 in range(p + 1):
            same = across[p] == down[p2]
            if p2 == p:
                same = same & earlier
            rank = rank + jnp.sum(jnp.where(same, 1.0, 0.0), axis=0, keepdims=True)
        ranks.append(rank)
    base = (((slab // 8) * 8 + piece) * 32 + (slab % 8) * 4).astype(F32)
    position = [base[p:p + 1, :] + ranks[p] for p in range(4)]
    key4 = ((slot % 64) * 4 + iota((4, 128), 0) + 1).astype(F32)
    keys = jnp.concatenate([key4[p:p + 1, :] for p in range(4)], axis=1)
    keys16 = jnp.broadcast_to(keys, (16, 512)).astype(BF16)
    mine16 = iota((16, 128), 0) == g % 16
    ins = rows_ins[...].astype(BF16)
    slot_iota = iota((128, 128), 0).astype(F32)

    def dispatch(chunk, _):
        where = slot_iota + (chunk * 128).astype(F32)
        pick = jnp.concatenate([jnp.where(where == position[p], 1.0, 0.0) for p in range(4)], axis=1).astype(BF16)
        data = dot(pick, ins).astype(BF16)
        meta = jnp.where(mine16, dot_nt(keys16, pick), 0.0).astype(BF16)
        for t in range(4):
            hop1_out[chunk * 4 + t, 0:32, :] = data[t * 32:(t + 1) * 32]
            hop1_out[chunk * 4 + t, 32:48, :] = meta
        return 0

    lax.fori_loop(0, 8, dispatch, 0)

    def h1_copy(i):
        to = g_peer(i)
        return copy(hop1_out.at[to], hop1_in.at[g], h1_send.at[i], h1_recv.at[i], (to // 8) * 8 + a, to % 8)

    lax.fori_loop(1, 32, lambda i, _: (h1_copy(i).start(), 0)[1], 0)
    hop1_in[g] = hop1_out[g]

    lax.fori_loop(1, 8, lambda i, _: (f_copy(i).wait_recv(), 0)[1], 0)

    def norms(q, _):
        q_hi = q + 32
        ky = jnp.where(odd8, -64, 0) + jnp.where(half8, q, q_hi)
        kyf = ky.astype(F32)
        radius = (kx2 + kyf * kyf) * (1.0 / 16384.0)
        n_lo = jnp.where(odd8, noise_full[pl.ds(q + 64, 1), :], noise_full[pl.ds(q, 1), :])
        n_hi = jnp.where(odd8, noise_full[pl.ds(q_hi + 64, 1), :], noise_full[pl.ds(q_hi, 1), :])
        outs_lo, outs_hi = [], []
        for b in range(8):
            squared = sine_squared(focus_in[b] * radius + 0.1)
            turned = pltpu.roll(squared, 64, 1)
            outs_lo.append(jnp.where(half8, squared, turned) * n_lo)
            outs_hi.append(jnp.where(half8, turned, squared) * n_hi)
        left_op[q, 192:256, 0:128] = jnp.concatenate(outs_lo, axis=0).astype(BF16)
        left_op[q, 192:256, 128:256] = jnp.concatenate(outs_hi, axis=0).astype(BF16)
        return 0

    lax.fori_loop(0, 32, norms, 0)

    lane16 = iota((16, 128), 1)
    angle_x = (lane16 % 64).astype(F32) * (2.0 * PI / 128.0)
    cos_x = sine(angle_x + 0.5 * PI)
    sin_x = sine(angle_x) * jnp.where(lane16 < 64, 1.0, -1.0)
    angle_y = iota((64, 128), 0).astype(F32) * (2.0 * PI / 128.0)
    turn_tab[0] = sine(angle_y + 0.5 * PI)
    turn_tab[1] = sine(angle_y) * jnp.where(iota((64, 128), 1) < 64, -1.0, 1.0)
    flip16 = jnp.where(iota((16, 128), 0) % 2 == 1, -1.0, 1.0)

    def views(block, begin, end):
        row = pl.multiple_of(block * 16, 16)

        def step(q, _):
            for h in range(2):
                qq = q + 32 * h
                image = proj_in[block, pl.ds(pl.multiple_of(qq * 16, 16), 16), :].astype(F32)
                lanes = pl.ds(h * 128, 128)
                u = image * (flip16 * turn_tab[0, pl.ds(qq, 1), :])
                v = pltpu.roll(image, 64, 1) * (flip16 * turn_tab[1, pl.ds(qq, 1), :])
                right_op[q, pl.ds(row, 16), lanes] = (u - v).astype(BF16)
                right_op[q, pl.ds(row + 64, 16), lanes] = image.astype(BF16)
                right_op[q, pl.ds(row + 128, 16), lanes] = (u + v).astype(BF16)
                right_op[q, pl.ds(row + 192, 16), lanes] = (image * image).astype(BF16)
            return 0

        lax.fori_loop(begin, end, step, 0, unroll=2)

    def turns(zz):
        row = pl.multiple_of(zz * 16, 16)

        def step(q2, _):
            for h in range(2):
                at = pl.ds(pl.multiple_of((q2 + 16 * h) * 16, 16), 16)
                first = weight_in[zz * 2, at, :].astype(F32)
                second = weight_in[zz * 2 + 1, at, :].astype(F32)
                lanes = pl.ds(h * 128, 128)
                for e in range(2):
                    image = jnp.concatenate([first[e * 8:e * 8 + 8], second[e * 8:e * 8 + 8]], axis=0)
                    u = image * cos_x
                    v = pltpu.roll(image, 64, 1) * sin_x
                    left_op[q2 * 2 + e, pl.ds(row, 16), lanes] = (u - v).astype(BF16)
                    left_op[q2 * 2 + e, pl.ds(row + 64, 16), lanes] = image.astype(BF16)
                    left_op[q2 * 2 + e, pl.ds(row + 128, 16), lanes] = (u + v).astype(BF16)
            return 0

        lax.fori_loop(0, 16, step, 0)

    from_left, from_right, across_x = (x + 3) % 4, (x + 1) % 4, (x + 2) % 4

    p_copy(0, from_left, top, right).wait_recv()
    p_copy(4, from_left, top, right).start()
    p_copy(2, from_right, low, left).wait_recv()
    p_copy(5, from_right, low, left).start()
    views(x, 0, 32)
    for i in (1, 3, 2):
        block = ((z + 4 - i) % 4) * 2 + core
        w_copy(i, block, a).wait_recv()
        w_copy(3 + i, block, z * 2 + 1 - core).start()
    w_copy(0, a, a).wait_recv()
    turns(z)
    p_copy(1, from_left, low, right).wait_recv()
    views(from_left, 0, 32)
    p_copy(3, from_right, top, left).wait_recv()
    views(from_right, 0, 32)

    lax.fori_loop(1, 32, lambda i, _: (h1_copy(i).wait_recv(), 0)[1], 0)
    o_row, o_col = iota((128, 128), 0), iota((128, 128), 1)
    mix = jnp.where(o_col == ((o_row // 4) % 4) * 32 + (o_row // 16) * 4 + o_row % 4, 1.0, 0.0).astype(BF16)

    def regroup(group, _):
        four = jnp.concatenate([hop1_in[group * 4 + t, 0:32, :] for t in range(4)], axis=0)
        mixed = dot(mix, four).astype(BF16)
        at = pl.ds(pl.multiple_of(group * 16, 16), 16)
        for b in range(8):
            hop2_out[b, at, :] = mixed[b * 16:(b + 1) * 16]
        return 0

    lax.fori_loop(0, 8, regroup, 0)
    key_rows = []
    for half in range(2):
        total = hop1_in[half * 16, 32:48, :].astype(F32)
        for t in range(1, 16):
            total = total + hop1_in[half * 16 + t, 32:48, :].astype(F32)
        key_rows.append(total)
    meta = jnp.concatenate(key_rows, axis=0).astype(BF16)
    for b in range(8):
        hop2_out[b, 128:160, :] = meta

    def h2_copy(i):
        to = a_peer(i)
        return copy(hop2_out.at[to], hop2_in.at[a], h2_send.at[i], h2_recv.at[i], x * 8 + to, dom)

    lax.fori_loop(1, 8, lambda i, _: (h2_copy(i).start(), 0)[1], 0)
    hop2_in[a] = hop2_out[a]

    for i in (1, 3, 2):
        block = ((z + 4 - i) % 4) * 2 + 1 - core
        w_copy(3 + i, block, a).wait_recv()
        turns((z + 4 - i) % 4)
    p_copy(4, across_x, top, right).wait_recv()
    p_copy(5, across_x, low, left).wait_recv()
    views(across_x, 0, 32)

    score[...] = jnp.zeros_like(score)

    def multiply(k, _):
        part = dot_nt(left_op[k], right_op[k])
        score[0] += part[:, 0:128]
        score[1] += part[:, 128:256]
        return 0

    lax.fori_loop(0, 32, multiply, 0, unroll=4)

    even = jnp.concatenate([score[h, pl.ds(0, 128, stride=2), :] for h in range(2)], axis=1)
    odd = jnp.concatenate([score[h, pl.ds(1, 128, stride=2), :] for h in range(2)], axis=1)
    folded = even + pltpu.roll(odd, 255, 1)
    lane32 = iota((32, 128), 1)
    penalty = folded[96:128, 128:256]
    penalty = 0.5 * jnp.where(lane32 < 64, pltpu.roll(penalty, 64, 1), penalty)
    penalty = jnp.concatenate([penalty, penalty], axis=1)
    lane = iota((32, 256), 1)
    valid = (lane % 2 == 0) & (lane < 192)
    scores = [jnp.where(valid, folded[s * 32:(s + 1) * 32, :] - penalty, -3e38) for s in range(3)]
    top_score = jnp.max(jnp.maximum(jnp.maximum(scores[0], scores[1]), scores[2]), axis=1, keepdims=True)
    weight = sum(jnp.where(valid, jnp.exp(s - top_score), 0.0) for s in scores)
    t_row, t_col = iota((256, 256), 0), iota((256, 256), 1)
    same_class = jnp.where((t_row // 2) % 8 == t_col % 8, 1.0, 0.0).astype(BF16)
    own = lane // 8 == iota((32, 256), 0)
    sums = jnp.sum(jnp.where(own, split_dot(weight, same_class), 0.0), axis=0, keepdims=True)
    tops = jnp.sum(jnp.where(own, top_score, 0.0), axis=0, keepdims=True)
    row8 = iota((8, 128), 0)
    tile = jnp.where(row8 == 0, sums[:, 0:128], 0.0)
    tile = jnp.where(row8 == 1, sums[:, 128:256], tile)
    tile = jnp.where(row8 == 2, tops[:, 0:128], tile)
    stat[a] = jnp.where(row8 == 3, tops[:, 128:256], tile)

    def s_copy(i):
        return copy(stat.at[a], stat.at[a], s_send.at[i], s_recv.at[i], x * 8 + a_peer(i), dom)

    lax.fori_loop(1, 8, lambda i, _: (s_copy(i).start(), 0)[1], 0)
    lax.fori_loop(1, 8, lambda i, _: (s_copy(i).wait_recv(), 0)[1], 0)
    best = stat[0]
    for b in range(1, 8):
        best = jnp.maximum(best, stat[b])
    total = jnp.zeros((8, 128), F32)
    for b in range(8):
        tile = stat[b]
        total = total + tile * pltpu.roll(jnp.exp(tile - best), 6, 0)
    total = jnp.where(row8 < 2, total, 0.0)
    same_particle = jnp.where(o_row // 8 == o_col // 8, 1.0, 0.0).astype(BF16)
    class_w = jnp.where(row8 < 2, total / split_dot(total, same_particle), 0.0)
    first, second = class_w[0:1, :], class_w[1:2, :]
    tile = jnp.where(row8 == (g % 4) * 2, first, 0.0)
    cwt[g] = jnp.where(row8 == (g % 4) * 2 + 1, second, tile)

    def c_copy(i):
        to = g_peer(i)
        return copy(cwt.at[g], cwt.at[g], c_send.at[i], c_recv.at[i], (to // 8) * 8 + a, to % 8)

    lax.fori_loop(1, 32, lambda i, _: (c_copy(i).start(), 0)[1], 0)

    flat = jnp.concatenate([first, second], axis=1)
    spread = jnp.where(iota((8, 256), 1) // 8 == iota((8, 256), 0) + a * 4, flat, 0.0)
    gather_class = jnp.where(iota((256, 128), 0) % 8 == iota((256, 128), 1), 1.0, 0.0).astype(BF16)
    hi = spread.astype(BF16)
    rest = spread - hi.astype(F32)
    cw_flat[...] = dot(hi, gather_class) + split_dot(rest, gather_class)
    cw_ref[...] = cw_flat[0:4, 0:8]

    lax.fori_loop(1, 8, lambda i, _: (h2_copy(i).wait_recv(), 0)[1], 0)
    lax.fori_loop(1, 32, lambda i, _: (c_copy(i).wait_recv(), 0)[1], 0)

    gathered = []
    for group in range(8):
        tile = cwt[group * 4]
        for t in range(1, 4):
            tile = tile + cwt[group * 4 + t]
        gathered.append(tile)
    table = jnp.concatenate(gathered + [jnp.zeros((64, 128), F32)], axis=0).T.astype(BF16)
    for half in range(2):
        repeat = jnp.where(o_row == (o_col // 4) * 2 + half, 1.0, 0.0).astype(BF16)
        coef_tab[half * 128:(half + 1) * 128, :] = dot(table, repeat)
    pick_key = jnp.where(o_row == (g % 4) * 32 + a * 4 + o_col % 4, 1.0, 0.0).astype(BF16)
    own_source = lane32 // 4 == iota((32, 128), 0)
    slot64 = iota((64, 128), 0).astype(F32)
    vol_ref[...] = jnp.zeros_like(vol_ref)

    def insert(pair, _):
        parts = []
        for h in range(2):
            source = pair * 2 + h
            keys_of = dot(hop2_in[source, 128:160, :], pick_key)
            key = jnp.sum(jnp.where(own_source, keys_of, 0.0), axis=0, keepdims=True) - 1.0
            at_slot = jnp.floor(key * 0.25)
            which = key - 4.0 * at_slot
            coef = jnp.zeros((8, 128), F32)
            for p in range(4):
                rows = pl.ds(pl.multiple_of(source * 32 + p * 8, 8), 8)
                coef = jnp.where(which == float(p), coef_tab[rows, :], coef)
            hit = slot64 == at_slot
            parts.append(
                jnp.concatenate([jnp.where(hit, coef[c:c + 1, :], 0.0) for c in range(8)], axis=0).astype(BF16)
            )
        rows_in = jnp.concatenate([hop2_in[pair * 2, 0:128, :], hop2_in[pair * 2 + 1, 0:128, :]], axis=0)
        vol_ref[...] += dot(jnp.concatenate(parts, axis=1), rows_in)
        return 0

    lax.fori_loop(0, 4, insert, 0)

    for k in range(6):
        p_copy(k, x, top, right).wait_send()
    for k in range(7):
        w_copy(k, a, a).wait_send()
    lax.fori_loop(1, 8, lambda i, _: (f_copy(i).wait_send(), h2_copy(i).wait_send(), s_copy(i).wait_send(), 0)[3], 0)
    lax.fori_loop(1, 32, lambda i, _: (h1_copy(i).wait_send(), c_copy(i).wait_send(), 0)[2], 0)


def per_device(particles, defocus, noise_weight, projections, row_slab, row_slot, interp):
    vmem, dma = pltpu.VMEM, pltpu.SemaphoreType.DMA
    focus = jnp.broadcast_to(jnp.repeat(defocus, 2)[:, None], (8, 128))
    volume, class_weight = pl.pallas_call(
        kernel,
        out_shape=(jax.ShapeDtypeStruct((512, 128), F32), jax.ShapeDtypeStruct((4, 8), F32)),
        in_specs=[pl.BlockSpec(memory_space=vmem)] * 7,
        out_specs=(pl.BlockSpec(memory_space=vmem), pl.BlockSpec(memory_space=vmem)),
        scratch_shapes=[
            vmem((512, 128), F32),
            vmem((1024, 128), F32),
            vmem((128, 128), F32),
            vmem((512, 128), F32),
            vmem((8, 512, 128), BF16),
            vmem((4, 1024, 128), BF16),
            vmem((8, 8, 128), F32),
            vmem((512, 128), F32),
            vmem((32, 256, 256), BF16),
            vmem((32, 256, 256), BF16),
            vmem((2, 256, 128), F32),
            vmem((2, 64, 128), F32),
            vmem((32, 48, 128), BF16),
            vmem((32, 48, 128), BF16),
            vmem((8, 160, 128), BF16),
            vmem((8, 160, 128), BF16),
            vmem((8, 8, 128), F32),
            vmem((32, 8, 128), F32),
            vmem((8, 128), F32),
            vmem((256, 128), F32),
            dma((7,)), dma((7,)), dma((6,)), dma((6,)), dma((8,)), dma((8,)), dma((32,)), dma((32,)),
            dma((8,)), dma((8,)), dma((8,)), dma((8,)), dma((32,)), dma((32,)),
        ],
        compiler_params=pltpu.CompilerParams(
            collective_id=0, has_side_effects=True, vmem_limit_bytes=40 * 1024 * 1024
        ),
    )(
        particles.reshape(512, 128), focus, noise_weight, projections.reshape(1024, 128),
        row_slab.reshape(4, 128), row_slot, interp,
    )
    return volume.reshape(8, 64, 128), class_weight


def solution(mesh):
    in_specs = (
        P(("blk", "dom"), None, None),
        P(("blk", "dom")),
        P(),
        P(None, "blk", None, None),
        P(("blk", "dom"), None, None),
        P(("blk", "dom"), None),
        P(("blk", "dom"), None),
    )
    out_specs = (P(None, ("blk", "dom"), None), P(("blk", "dom"), None))
    return jax.shard_map(per_device, mesh=mesh, in_specs=in_specs, out_specs=out_specs, check_vma=False)
```

```python
import jax
import jax.numpy as jnp
from jax import lax
from jax.experimental import pallas as pl
from jax.experimental.pallas import tpu as pltpu
from jax.sharding import PartitionSpec as P

F32, BF16 = jnp.float32, jnp.bfloat16
MESH = pl.DeviceIdType.MESH
PI = 3.141592653589793
SIN_COEF = (
    0.9999999992267364, -0.16666665898756483, 0.008333320916259667, -0.00019840515744570079,
    2.7535452887970435e-06, -2.47248903062851e-08, 1.3598699876951359e-10,
)
SIN2_COEF = (
    0.9999999902438815, -0.3333330511544617, 0.044443119935340766, -0.00317232337316227,
    0.00013931019440764148, -3.6240280738953943e-06,
)


def reduced(angle, period, high, mid):
    turns = jnp.floor(angle * (1.0 / period) + 0.5)
    return ((angle - turns * high) - turns * mid) - turns * (period - high - mid)


def horner(coef, y):
    total = jnp.full_like(y, coef[-1])
    for c in coef[-2::-1]:
        total = total * y + c
    return total


def sine(angle):
    r = reduced(angle, 2 * PI, 6.28125, 8117 / 2**22)
    return r * horner(SIN_COEF, r * r)


def sine_squared(angle):
    r = reduced(angle, PI, 3.140625, 8117 / 2**23)
    y = r * r
    return y * horner(SIN2_COEF, y)


def iota(shape, axis):
    return lax.broadcasted_iota(jnp.int32, shape, axis)


def dot(a, b):
    return jnp.dot(a, b, preferred_element_type=F32)


def dot_nt(a, b):
    return lax.dot_general(a, b, (((1,), (1,)), ((), ())), preferred_element_type=F32)


def split_dot(values, indicator):
    high = values.astype(BF16)
    low = (values - high.astype(F32)).astype(BF16)
    return dot(high, indicator) + dot(low, indicator)


def kernel(
    part_hbm, focus_hbm, noise_hbm, proj_hbm, slab_hbm, slot_hbm, interp_hbm,
    vol_ref, cw_ref,
    part_ref, focus_ref, noise_ref, proj_ref, slab_ref, slot_ref, interp_ref,
    wide_p, wide_x, noise_full, cols, weight_in, proj_in, focus_in, rows_ins,
    left_op, right_op, score, turn_tab, hop1_out, hop1_in, hop2_out, hop2_in, stat, cwt, cw_flat, coef_tab,
    in_sem, w_send, w_recv, t_send, t_recv, p_send, p_recv, f_send, f_recv, h1_send, h1_recv, h2_send, h2_recv,
    s_send, s_recv, c_send, c_recv,
):
    blk, dom = lax.axis_index("blk"), lax.axis_index("dom")
    x, a = blk // 8, blk % 8
    z, core = a // 2, a % 2
    y, z_hi = dom // 2, dom % 2
    u = x * 4 + y
    v = z_hi * 8 + a
    g = z_hi * 16 + u

    def copy(src, dst, send, recv, to_blk, to_dom):
        return pltpu.make_async_remote_copy(
            src_ref=src, dst_ref=dst, send_sem=send, recv_sem=recv,
            device_id=(to_blk, to_dom), device_id_type=MESH,
        )

    def fetch(k, src, dst):
        return pltpu.make_async_copy(src, dst, in_sem.at[k])

    fetches = [
        fetch(0, part_hbm, part_ref), fetch(1, focus_hbm, focus_ref), fetch(2, noise_hbm, noise_ref),
        fetch(3, interp_hbm, interp_ref), fetch(4, proj_hbm, proj_ref), fetch(5, slab_hbm, slab_ref),
        fetch(6, slot_hbm, slot_ref),
    ]
    for f in fetches:
        f.start()

    def alpha(i):
        return x * 8 + (a + i) % 8, dom

    def gamma(i):
        to = (g + i) % 32
        return ((to % 16) // 4) * 8 + a, (to % 4) * 2 + to // 16

    def plane(i):
        to = (u + i) % 16
        return (to // 4) * 8 + a, (to % 4) * 2 + z_hi

    def column(i):
        to = (v + i) % 16
        return x * 8 + to % 8, y * 2 + to // 8

    barrier = pltpu.get_barrier_semaphore()

    def greet(who):
        def send(i, _):
            pl.semaphore_signal(barrier, inc=1, device_id=who(i), device_id_type=MESH)
            return 0
        return send

    lax.fori_loop(1, 16, greet(column), 0)
    lax.fori_loop(1, 32, greet(gamma), 0)

    def p_copy(k, block, part, to):
        rows = pl.ds(part * 256, 256)
        return copy(proj_in.at[block, rows], proj_in.at[block, rows], p_send.at[k], p_recv.at[k], to, dom)

    def w_copy(k, block, half, to):
        rows = pl.ds(half * 256, 256)
        return copy(
            weight_in.at[block, rows], weight_in.at[block, rows], w_send.at[k * 2 + half],
            w_recv.at[(block // 2) * 2 + half], x * 8 + to, dom,
        )

    def t_copy(block, half):
        rows = pl.ds(half * 256, 256)
        k = (block // 2) * 2 + half
        return copy(
            weight_in.at[block, rows], weight_in.at[block, rows], t_send.at[k], t_recv.at[k],
            x * 8 + z * 2 + 1 - core, dom,
        )

    right, left = ((x + 1) % 4) * 8 + a, ((x + 3) % 4) * 8 + a
    from_left, from_right, across_x = (x + 3) % 4, (x + 1) % 4, (x + 2) % 4

    def to_right(part):
        return p_copy(part, x, part, right)

    def to_left(part):
        return p_copy(4 + part, x, part, left)

    def came_left(part):
        return p_copy(part, from_left, part, right)

    def came_right(part):
        return p_copy(4 + part, from_right, part, left)

    def pass_right(part):
        return p_copy(8 + part, from_left, part, right)

    def pass_left(part):
        return p_copy(8 + part, from_right, part, left)

    def came_across(part):
        return p_copy(8 + part, across_x, part, right)

    def each_z(act):
        for away in (2, 1):
            for sign in (1, -1):
                target = z + sign * away

                @pl.when((target >= 0) & (target < 4))
                def _():
                    act(target)

    relays = (z == 1) | (z == 2)
    relay_from, relay_to = (2 - z) * 3, (z - 1) * 3

    lane8 = iota((8, 128), 1)
    row8 = iota((8, 128), 0)
    kx = (lane8 % 64).astype(F32)
    kx2 = kx * kx
    odd8 = (row8 % 2) == 1
    half8 = lane8 < 64

    for k in (1, 2, 3):
        fetches[k].wait()
    noise_half = noise_ref[...]
    noise_full[...] = jnp.concatenate([noise_half, noise_half], axis=0).T
    interp = interp_ref[...]
    for p in range(4):
        cols[p * 128:(p + 1) * 128, :] = jnp.broadcast_to(interp[p:p + 1, :], (128, 128)).T
    lane4 = iota((8, 4), 1)
    focus4 = jnp.broadcast_to(focus_ref[...], (8, 4))
    focus = jnp.sum(jnp.where(lane4 == iota((8, 4), 0) // 2, focus4, 0.0), axis=1, keepdims=True)
    focus = jnp.broadcast_to(focus, (8, 128))
    focus_in[a] = focus
    fetches[0].wait()
    wide_p[...] = part_ref[...].astype(F32)

    def weigh(q2, _):
        tiles = []
        for h in range(2):
            q = q2 * 2 + h
            rows = pl.ds(q, 8, stride=64)
            image = wide_p[rows, :]
            ky = jnp.where(odd8, q - 64, q).astype(F32)
            radius = (kx2 + ky * ky) * (1.0 / 16384.0)
            signal = -sine(focus * radius + 0.1) * image
            noise = jnp.where(odd8, noise_full[pl.ds(q + 64, 1), :], noise_full[pl.ds(q, 1), :])
            tiles.append(signal * noise)
            rows_ins[rows, :] = signal * cols[rows, :]
        weight_in[a, pl.ds(pl.multiple_of(q2 * 16, 16), 16), :] = jnp.concatenate(tiles, axis=0).astype(BF16)
        return 0

    def order_proj(q, _):
        tile = wide_x[pl.ds(q, 16, stride=64), :].astype(BF16)
        proj_in[x, pl.ds(pl.multiple_of(q * 16, 16), 16), :] = tile
        return 0

    def f_copy(i):
        to = alpha(i)
        return copy(focus_in.at[a], focus_in.at[a], f_send.at[i], f_recv.at[i], to[0], to[1])

    lax.fori_loop(0, 16, weigh, 0, unroll=4)
    pl.semaphore_wait(barrier, 46)
    each_z(lambda target: w_copy(target, a, 0, target * 2 + core).start())
    t_copy(a, 0).start()
    fetches[4].wait()
    wide_x[...] = proj_ref[...].astype(F32)
    lax.fori_loop(0, 32, order_proj, 0, unroll=8)
    to_right(0).start()
    to_left(1).start()
    to_right(1).start()
    to_left(0).start()
    lax.fori_loop(1, 8, lambda i, _: (f_copy(i).start(), 0)[1], 0)
    lax.fori_loop(16, 32, weigh, 0, unroll=4)
    each_z(lambda target: w_copy(target, a, 1, target * 2 + core).start())
    t_copy(a, 1).start()
    lax.fori_loop(32, 64, order_proj, 0, unroll=8)
    to_right(2).start()
    to_left(3).start()
    to_right(3).start()
    to_left(2).start()

    fetches[5].wait()
    fetches[6].wait()
    slab, slot = slab_ref[...], slot_ref[...]
    piece = slot // 64
    bucket = (slab * 8 + piece).astype(F32)
    earlier = iota((128, 128), 0) < iota((128, 128), 1)
    ranks = []
    across = [jnp.broadcast_to(bucket[p:p + 1, :], (128, 128)) for p in range(4)]
    down = [b.T for b in across]
    for p in range(4):
        rank = jnp.zeros((1, 128), F32)
        for p2 in range(p + 1):
            same = across[p] == down[p2]
            if p2 == p:
                same = same & earlier
            rank = rank + jnp.sum(jnp.where(same, 1.0, 0.0), axis=0, keepdims=True)
        ranks.append(rank)
    to_plane = (slab // 8) * 4 + piece // 2
    to_column = (piece % 2) * 8 + slab % 8
    base = (to_plane * 64 + to_column * 4).astype(F32)
    position = [base[p:p + 1, :] + ranks[p] for p in range(4)]
    key4 = ((slot % 64) * 4 + iota((4, 128), 0) + 1).astype(F32)
    keys = jnp.concatenate([key4[p:p + 1, :] for p in range(4)], axis=1)
    keys16 = jnp.broadcast_to(keys, (16, 512)).astype(BF16)
    mine16 = iota((16, 128), 0) == u
    ins = rows_ins[...].astype(BF16)
    slot_iota = iota((128, 128), 0).astype(F32)

    def dispatch(chunk, _):
        where = slot_iota + (chunk * 128).astype(F32)
        pick = jnp.concatenate([jnp.where(where == position[p], 1.0, 0.0) for p in range(4)], axis=1).astype(BF16)
        data = dot(pick, ins).astype(BF16)
        meta = jnp.where(mine16, dot_nt(keys16, pick), 0.0).astype(BF16)
        for t in range(2):
            hop1_out[chunk * 2 + t, 0:64, :] = data[t * 64:(t + 1) * 64]
            hop1_out[chunk * 2 + t, 64:80, :] = meta
        return 0

    lax.fori_loop(0, 8, dispatch, 0, unroll=2)

    def h1_copy(i):
        to = plane(i)
        return copy(hop1_out.at[(u + i) % 16], hop1_in.at[u], h1_send.at[i], h1_recv.at[i], to[0], to[1])

    lax.fori_loop(1, 16, lambda i, _: (h1_copy(i).start(), 0)[1], 0)
    hop1_in[u] = hop1_out[u]

    def pass_proj(half):
        came_left(2 * half).wait_recv()
        pass_right(2 * half).start()
        came_right(2 * half + 1).wait_recv()
        pass_left(2 * half + 1).start()

    def pass_weight(half):
        @pl.when(relays)
        def _():
            w_copy(relay_from, relay_from * 2 + core, half, a).wait_recv()
            w_copy(z, relay_from * 2 + core, half, relay_to * 2 + core).start()
            t_copy(relay_from * 2 + core, half).start()

        for i in range(1, 4):
            source = (z + i) % 4

            @pl.when(jnp.logical_not(relays & (source == relay_from)))
            def _():
                w_copy(source, source * 2 + core, half, a).wait_recv()
                t_copy(source * 2 + core, half).start()

    def norms(k, _):
        low_tiles, high_tiles = [], []
        for e in range(8):
            q = k * 8 + e
            q_hi = q + 32
            ky = (jnp.where(odd8, -64, 0) + jnp.where(half8, q, q_hi)).astype(F32)
            radius = (kx2 + ky * ky) * (1.0 / 16384.0)
            n_lo = jnp.where(odd8, noise_full[pl.ds(q + 64, 1), :], noise_full[pl.ds(q, 1), :])
            n_hi = jnp.where(odd8, noise_full[pl.ds(q_hi + 64, 1), :], noise_full[pl.ds(q_hi, 1), :])
            outs_lo, outs_hi = [], []
            for b in range(8):
                squared = sine_squared(focus_in[b] * radius + 0.1)
                turned = pltpu.roll(squared, 64, 1)
                outs_lo.append(jnp.where(half8, squared, turned) * n_lo)
                outs_hi.append(jnp.where(half8, turned, squared) * n_hi)
            lanes = pl.ds(e * 128, 128)
            left_op[k, 192:256, lanes] = jnp.concatenate(outs_lo, axis=0).astype(BF16)
            left_op[k + 4, 192:256, lanes] = jnp.concatenate(outs_hi, axis=0).astype(BF16)
        return 0

    lane16 = iota((16, 128), 1)
    angle_x = (lane16 % 64).astype(F32) * (2.0 * PI / 128.0)
    cos_x = sine(angle_x + 0.5 * PI)
    sin_x = sine(angle_x) * jnp.where(lane16 < 64, 1.0, -1.0)
    angle_y = iota((64, 128), 0).astype(F32) * (2.0 * PI / 128.0)
    turn_tab[0] = sine(angle_y + 0.5 * PI)
    turn_tab[1] = sine(angle_y) * jnp.where(iota((64, 128), 1) < 64, -1.0, 1.0)
    flip16 = jnp.where(iota((16, 128), 0) % 2 == 1, -1.0, 1.0)

    def views(block, half):
        row = pl.multiple_of(block * 16, 16)

        def step(k, _):
            for e in range(8):
                q = k * 8 + e
                image_half = proj_in[block, pl.ds(pl.multiple_of(q * 16, 16), 16), :]
                image = image_half.astype(F32)
                lanes = pl.ds(e * 128, 128)
                w = image * (flip16 * turn_tab[0, pl.ds(q, 1), :])
                s = pltpu.roll(image, 64, 1) * (flip16 * turn_tab[1, pl.ds(q, 1), :])
                right_op[k, pl.ds(row, 16), lanes] = (w - s).astype(BF16)
                right_op[k, pl.ds(row + 64, 16), lanes] = image_half
                right_op[k, pl.ds(row + 128, 16), lanes] = (w + s).astype(BF16)
                right_op[k, pl.ds(row + 192, 16), lanes] = (image * image).astype(BF16)
            return 0

        lax.fori_loop(half * 4, half * 4 + 4, step, 0)

    def turns(zz, half):
        row = pl.multiple_of(zz * 16, 16)

        def step(k, _):
            for e2 in range(4):
                at = pl.ds(pl.multiple_of(k * 64 + e2 * 16, 16), 16)
                first = weight_in[zz * 2, at, :].astype(F32)
                second = weight_in[zz * 2 + 1, at, :].astype(F32)
                for e in range(2):
                    lanes = pl.ds((e2 * 2 + e) * 128, 128)
                    image = jnp.concatenate([first[e * 8:e * 8 + 8], second[e * 8:e * 8 + 8]], axis=0)
                    w = image * cos_x
                    s = pltpu.roll(image, 64, 1) * sin_x
                    left_op[k, pl.ds(row, 16), lanes] = (w - s).astype(BF16)
                    left_op[k, pl.ds(row + 64, 16), lanes] = image.astype(BF16)
                    left_op[k, pl.ds(row + 128, 16), lanes] = (w + s).astype(BF16)
            return 0

        lax.fori_loop(half * 4, half * 4 + 4, step, 0)

    def multiply(half):
        part = dot_nt(left_op[half * 4], right_op[half * 4])
        for k in range(1, 4):
            part = part + dot_nt(left_op[half * 4 + k], right_op[half * 4 + k])
        for h in range(2):
            lanes = part[:, h * 128:(h + 1) * 128]
            score[h] = lanes if half == 0 else score[h] + lanes

    pass_proj(0)
    lax.fori_loop(1, 8, lambda i, _: (f_copy(i).wait_recv(), 0)[1], 0)
    lax.fori_loop(0, 2, norms, 0)
    pass_weight(0)
    views(x, 0)
    lax.fori_loop(2, 4, norms, 0)
    pass_proj(1)
    views(x, 1)
    t_copy(a, 0).wait_recv()
    turns(z, 0)
    pass_weight(1)

    lax.fori_loop(1, 16, lambda i, _: (h1_copy(i).wait_recv(), 0)[1], 0)
    m_row, m_col = iota((256, 256), 0), iota((256, 256), 1)
    mix = jnp.where(m_col == ((m_row // 4) % 4) * 64 + (m_row // 16) * 4 + m_row % 4, 1.0, 0.0).astype(BF16)

    def regroup(group, _):
        four = jnp.concatenate([hop1_in[group * 4 + t, 0:64, :] for t in range(4)], axis=0)
        mixed = dot(mix, four).astype(BF16)
        at = pl.ds(pl.multiple_of(group * 16, 16), 16)
        for b in range(16):
            hop2_out[b, at, :] = mixed[b * 16:(b + 1) * 16]
        return 0

    lax.fori_loop(0, 4, regroup, 0)
    meta = hop1_in[0, 64:80, :].astype(F32)
    for t in range(1, 16):
        meta = meta + hop1_in[t, 64:80, :].astype(F32)
    meta = meta.astype(BF16)
    for b in range(16):
        hop2_out[b, 64:80, :] = meta

    def h2_copy(i):
        to = column(i)
        return copy(hop2_out.at[(v + i) % 16], hop2_in.at[v], h2_send.at[i], h2_recv.at[i], to[0], to[1])

    lax.fori_loop(1, 16, lambda i, _: (h2_copy(i).start(), 0)[1], 0)
    hop2_in[v] = hop2_out[v]

    came_left(1).wait_recv()
    came_right(0).wait_recv()
    views(from_left, 0)
    views(from_right, 0)
    for i in range(1, 4):
        source = (z + i) % 4
        t_copy(source * 2 + 1 - core, 0).wait_recv()
        turns(source, 0)
    came_across(0).wait_recv()
    came_across(1).wait_recv()
    views(across_x, 0)
    multiply(0)
    t_copy(a, 1).wait_recv()
    turns(z, 1)
    came_left(3).wait_recv()
    came_right(2).wait_recv()
    views(from_left, 1)
    views(from_right, 1)
    came_across(2).wait_recv()
    came_across(3).wait_recv()
    views(across_x, 1)
    for i in range(1, 4):
        source = (z + i) % 4
        t_copy(source * 2 + 1 - core, 1).wait_recv()
        turns(source, 1)
    multiply(1)

    even = jnp.concatenate([score[h, pl.ds(0, 128, stride=2), :] for h in range(2)], axis=1)
    odd = jnp.concatenate([score[h, pl.ds(1, 128, stride=2), :] for h in range(2)], axis=1)
    folded = even + pltpu.roll(odd, 255, 1)
    lane32 = iota((32, 128), 1)
    penalty = folded[96:128, 128:256]
    penalty = 0.5 * jnp.where(lane32 < 64, pltpu.roll(penalty, 64, 1), penalty)
    penalty = jnp.concatenate([penalty, penalty], axis=1)
    lane = iota((32, 256), 1)
    valid = (lane % 2 == 0) & (lane < 192)
    scores = [jnp.where(valid, folded[s * 32:(s + 1) * 32, :] - penalty, -3e38) for s in range(3)]
    top_score = jnp.max(jnp.maximum(jnp.maximum(scores[0], scores[1]), scores[2]), axis=1, keepdims=True)
    weight = sum(jnp.where(valid, jnp.exp(s - top_score), 0.0) for s in scores)
    same_class = jnp.where((m_row // 2) % 8 == m_col % 8, 1.0, 0.0).astype(BF16)
    own = lane // 8 == iota((32, 256), 0)
    sums = jnp.sum(jnp.where(own, split_dot(weight, same_class), 0.0), axis=0, keepdims=True)
    tops = jnp.sum(jnp.where(own, top_score, 0.0), axis=0, keepdims=True)
    tile = jnp.where(row8 == 0, sums[:, 0:128], 0.0)
    tile = jnp.where(row8 == 1, sums[:, 128:256], tile)
    tile = jnp.where(row8 == 2, tops[:, 0:128], tile)
    stat[a] = jnp.where(row8 == 3, tops[:, 128:256], tile)

    def s_copy(i):
        to = alpha(i)
        return copy(stat.at[a], stat.at[a], s_send.at[i], s_recv.at[i], to[0], to[1])

    for i in range(1, 8):
        s_copy(i).start()

    for part in range(4):
        to_right(part).wait_send()
        to_left(part).wait_send()
    for half in range(2):
        pass_right(2 * half).wait_send()
        pass_left(2 * half + 1).wait_send()
        each_z(lambda target: w_copy(target, a, half, target * 2 + core).wait_send())

        @pl.when(relays)
        def _():
            w_copy(z, relay_from * 2 + core, half, relay_to * 2 + core).wait_send()

        for zz in range(4):
            t_copy(zz * 2 + core, half).wait_send()
    lax.fori_loop(1, 8, lambda i, _: (f_copy(i).wait_send(), 0)[1], 0)
    lax.fori_loop(1, 16, lambda i, _: (h1_copy(i).wait_send(), 0)[1], 0)

    for i in range(1, 8):
        s_copy(i).wait_recv()
    best = stat[0]
    for b in range(1, 8):
        best = jnp.maximum(best, stat[b])
    total = jnp.zeros((8, 128), F32)
    for b in range(8):
        tile = stat[b]
        total = total + tile * pltpu.roll(jnp.exp(tile - best), 6, 0)
    total = jnp.where(row8 < 2, total, 0.0)
    o_row, o_col = iota((128, 128), 0), iota((128, 128), 1)
    same_particle = jnp.where(o_row // 8 == o_col // 8, 1.0, 0.0).astype(BF16)
    class_w = jnp.where(row8 < 2, total / split_dot(total, same_particle), 0.0)
    first, second = class_w[0:1, :], class_w[1:2, :]
    tile = jnp.where(row8 == (u % 4) * 2, first, 0.0)
    cwt[g] = jnp.where(row8 == (u % 4) * 2 + 1, second, tile)

    def c_copy(i):
        to = gamma(i)
        return copy(cwt.at[g], cwt.at[g], c_send.at[i], c_recv.at[i], to[0], to[1])

    for i in range(1, 32):
        c_copy(i).start()

    flat = jnp.concatenate([first, second], axis=1)
    spread = jnp.where(iota((8, 256), 1) // 8 == iota((8, 256), 0) + a * 4, flat, 0.0)
    gather_class = jnp.where(iota((256, 128), 0) % 8 == iota((256, 128), 1), 1.0, 0.0).astype(BF16)
    hi = spread.astype(BF16)
    rest = spread - hi.astype(F32)
    cw_flat[...] = dot(hi, gather_class) + split_dot(rest, gather_class)
    cw_ref[...] = cw_flat[0:4, 0:8]

    for i in range(1, 8):
        s_copy(i).wait_send()
    lax.fori_loop(1, 16, lambda i, _: (h2_copy(i).wait_send(), 0)[1], 0)
    lax.fori_loop(1, 16, lambda i, _: (h2_copy(i).wait_recv(), 0)[1], 0)
    pick_key = jnp.where(o_row == (u % 2) * 64 + v * 4 + o_col % 4, 1.0, 0.0).astype(BF16)
    own_source = lane32 // 4 == iota((32, 128), 0)
    slot64 = iota((64, 128), 0).astype(F32)
    repeats = [
        jnp.where(o_row == (t // 2) * 32 + ((o_col % 64) // 4) * 2 + t % 2, 1.0, 0.0).astype(BF16) for t in range(4)
    ]
    lax.fori_loop(1, 32, lambda i, _: (c_copy(i).wait_recv(), 0)[1], 0)

    gathered = []
    for group in range(8):
        tile = cwt[group * 4]
        for t in range(1, 4):
            tile = tile + cwt[group * 4 + t]
        gathered.append(tile)
    table = jnp.concatenate(gathered + [jnp.zeros((64, 128), F32)], axis=0).T.astype(BF16)
    for t in range(4):
        coef_tab[t] = dot(table, repeats[t])
    vol_ref[...] = jnp.zeros_like(vol_ref)

    def insert(quad, _):
        parts, rows_in = [], []
        for h in range(2):
            w = quad * 2 + h
            tags = jnp.concatenate([hop2_in[w * 2, 64:80, :], hop2_in[w * 2 + 1, 64:80, :]], axis=0)
            key = jnp.sum(jnp.where(own_source, dot(tags, pick_key), 0.0), axis=0, keepdims=True) - 1.0
            at_slot = jnp.floor(key * 0.25)
            which = key - 4.0 * at_slot
            coef = jnp.zeros((8, 128), F32)
            for p in range(4):
                even_core = coef_tab[quad, h * 64 + p * 8:h * 64 + p * 8 + 8, :]
                odd_core = coef_tab[quad, h * 64 + 32 + p * 8:h * 64 + 40 + p * 8, :]
                coef = jnp.where(which == float(p), jnp.where(half8, even_core, odd_core), coef)
            hit = slot64 == at_slot
            parts.append(
                jnp.concatenate([jnp.where(hit, coef[c:c + 1, :], 0.0) for c in range(8)], axis=0).astype(BF16)
            )
            rows_in += [hop2_in[w * 2, 0:64, :], hop2_in[w * 2 + 1, 0:64, :]]
        vol_ref[...] += dot(jnp.concatenate(parts, axis=1), jnp.concatenate(rows_in, axis=0))
        return 0

    lax.fori_loop(0, 4, insert, 0)
    lax.fori_loop(1, 32, lambda i, _: (c_copy(i).wait_send(), 0)[1], 0)


def per_device(particles, defocus, noise_weight, projections, row_slab, row_slot, interp):
    vmem, dma = pltpu.VMEM, pltpu.SemaphoreType.DMA
    volume, class_weight = pl.pallas_call(
        kernel,
        out_shape=(jax.ShapeDtypeStruct((512, 128), F32), jax.ShapeDtypeStruct((4, 8), F32)),
        in_specs=[pl.BlockSpec(memory_space=pl.ANY)] * 7,
        out_specs=(pl.BlockSpec(memory_space=vmem), pl.BlockSpec(memory_space=vmem)),
        scratch_shapes=[
            vmem((512, 128), BF16),
            vmem((1, 4), F32),
            vmem((64, 128), F32),
            vmem((1024, 128), BF16),
            vmem((4, 128), jnp.int32),
            vmem((4, 128), jnp.int32),
            vmem((4, 128), F32),
            vmem((512, 128), F32),
            vmem((1024, 128), F32),
            vmem((128, 128), F32),
            vmem((512, 128), F32),
            vmem((8, 512, 128), BF16),
            vmem((4, 1024, 128), BF16),
            vmem((8, 8, 128), F32),
            vmem((512, 128), F32),
            vmem((8, 256, 1024), BF16),
            vmem((8, 256, 1024), BF16),
            vmem((2, 256, 128), F32),
            vmem((2, 64, 128), F32),
            vmem((16, 80, 128), BF16),
            vmem((16, 80, 128), BF16),
            vmem((16, 80, 128), BF16),
            vmem((16, 80, 128), BF16),
            vmem((8, 8, 128), F32),
            vmem((32, 8, 128), F32),
            vmem((8, 128), F32),
            vmem((4, 128, 128), F32),
            dma((7,)), dma((8,)), dma((8,)), dma((8,)), dma((8,)), dma((12,)), dma((12,)), dma((8,)), dma((8,)),
            dma((16,)), dma((16,)), dma((16,)), dma((16,)), dma((8,)), dma((8,)), dma((32,)), dma((32,)),
        ],
        compiler_params=pltpu.CompilerParams(
            collective_id=0, has_side_effects=True, vmem_limit_bytes=56 * 1024 * 1024
        ),
    )(
        particles.reshape(512, 128), defocus.reshape(1, 4), noise_weight.T, projections.reshape(1024, 128),
        row_slab.reshape(4, 128), row_slot, interp,
    )
    return volume.reshape(8, 64, 128), class_weight


def solution(mesh):
    in_specs = (
        P(("blk", "dom"), None, None),
        P(("blk", "dom")),
        P(),
        P(None, "blk", None, None),
        P(("blk", "dom"), None, None),
        P(("blk", "dom"), None),
        P(("blk", "dom"), None),
    )
    out_specs = (P(None, ("blk", "dom"), None), P(("blk", "dom"), None))
    return jax.shard_map(per_device, mesh=mesh, in_specs=in_specs, out_specs=out_specs, check_vma=False)
```

```python
import jax
import jax.numpy as jnp
from jax import lax
from jax.experimental import pallas as pl
from jax.experimental.pallas import tpu as pltpu
from jax.sharding import PartitionSpec as P

F32, BF16 = jnp.float32, jnp.bfloat16
MESH = pl.DeviceIdType.MESH
PI = 3.141592653589793
SIN_COEF = (
    0.9999999992267364, -0.16666665898756483, 0.008333320916259667, -0.00019840515744570079,
    2.7535452887970435e-06, -2.47248903062851e-08, 1.3598699876951359e-10,
)
SIN2_COEF = (
    0.9999999902438815, -0.3333330511544617, 0.044443119935340766, -0.00317232337316227,
    0.00013931019440764148, -3.6240280738953943e-06,
)


def reduced(angle, period, high, mid):
    turns = jnp.floor(angle * (1.0 / period) + 0.5)
    return ((angle - turns * high) - turns * mid) - turns * (period - high - mid)


def horner(coef, y):
    total = jnp.full_like(y, coef[-1])
    for c in coef[-2::-1]:
        total = total * y + c
    return total


def sine(angle):
    r = reduced(angle, 2 * PI, 6.28125, 8117 / 2**22)
    return r * horner(SIN_COEF, r * r)


def sine_squared(angle):
    r = reduced(angle, PI, 3.140625, 8117 / 2**23)
    y = r * r
    return y * horner(SIN2_COEF, y)


def iota(shape, axis):
    return lax.broadcasted_iota(jnp.int32, shape, axis)


def dot(a, b):
    return jnp.dot(a, b, preferred_element_type=F32)


def dot_nt(a, b):
    return lax.dot_general(a, b, (((1,), (1,)), ((), ())), preferred_element_type=F32)


def split_dot(values, indicator):
    high = values.astype(BF16)
    low = (values - high.astype(F32)).astype(BF16)
    return dot(high, indicator) + dot(low, indicator)


def kernel(
    part_hbm, focus_hbm, noise_hbm, proj_hbm, slab_hbm, slot_hbm, interp_hbm,
    vol_ref, cw_ref,
    part_ref, focus_ref, noise_ref, proj_ref, slab_ref, slot_ref, interp_ref,
    wide_p, wide_x, noise_full, cols, weight_in, proj_in, rows_ins,
    left_op, right_op, score, turn_tab, hop1_out, hop1_in, hop2_out, hop2_in,
    stat, cw_in, cw_flat, coef_tab,
    in_sem, w_send, w_recv, t_send, t_recv, p_send, p_recv, h1_send, h1_recv, h2_send, h2_recv,
    s_send, s_recv, c_send, c_recv,
):
    blk, dom = lax.axis_index("blk"), lax.axis_index("dom")
    x, a = blk // 8, blk % 8
    z, core = a // 2, a % 2
    y, z_hi = dom // 2, dom % 2
    u = x * 4 + y
    z_full = z_hi * 4 + z
    v = z_full * 2 + core

    def copy(src, dst, send, recv, to_blk, to_dom):
        return pltpu.make_async_remote_copy(
            src_ref=src, dst_ref=dst, send_sem=send, recv_sem=recv,
            device_id=(to_blk, to_dom), device_id_type=MESH,
        )

    def fetch(k, src, dst):
        return pltpu.make_async_copy(src, dst, in_sem.at[k])

    fetches = [
        fetch(0, part_hbm, part_ref), fetch(1, focus_hbm, focus_ref), fetch(2, noise_hbm, noise_ref),
        fetch(3, interp_hbm, interp_ref), fetch(4, proj_hbm, proj_ref), fetch(5, slab_hbm, slab_ref),
        fetch(6, slot_hbm, slot_ref),
    ]
    for f in fetches:
        f.start()

    other = x * 8 + z * 2 + 1 - core

    def plane(i):
        to = (u + i) % 16
        return (to // 4) * 8 + a, (to % 4) * 2 + z_hi

    def column(i):
        to = (v + i) % 16
        return x * 8 + to % 8, y * 2 + to // 8

    barrier = pltpu.get_barrier_semaphore()

    def greet(who):
        def send(i, _):
            pl.semaphore_signal(barrier, inc=1, device_id=who(i), device_id_type=MESH)
            return 0

        return send

    right, left = ((x + 1) % 4) * 8 + a, ((x + 3) % 4) * 8 + a
    from_left, from_right, across_x = (x + 3) % 4, (x + 1) % 4, (x + 2) % 4
    lax.fori_loop(1, 16, greet(column), 0)
    lax.fori_loop(1, 16, greet(plane), 0)

    def p_copy(k, block, part, to):
        rows = pl.ds(part * 512, 512)
        return copy(proj_in.at[block, rows], proj_in.at[block, rows], p_send.at[k], p_recv.at[k], to, dom)

    def to_right(part):
        return p_copy(part, x, part, right)

    def to_left(part):
        return p_copy(2 + part, x, part, left)

    def came_left(part):
        return p_copy(part, from_left, part, right)

    def came_right(part):
        return p_copy(2 + part, from_right, part, left)

    def pass_right():
        return p_copy(4, from_left, 0, right)

    def pass_left():
        return p_copy(5, from_right, 1, left)

    def w_copy(k, block, to):
        return copy(
            weight_in.at[block], weight_in.at[block], w_send.at[k], w_recv.at[block // 2], x * 8 + to, dom
        )

    def t_copy(block):
        return copy(
            weight_in.at[block], weight_in.at[block], t_send.at[block // 2], t_recv.at[block // 2], other, dom
        )

    def each_z(act):
        for away in (2, 1):
            for sign in (1, -1):
                target = z + sign * away

                @pl.when((target >= 0) & (target < 4))
                def _():
                    act(target)

    relays = (z == 1) | (z == 2)
    relay_from, relay_to = (2 - z) * 3, (z - 1) * 3

    lane8 = iota((8, 128), 1)
    row8 = iota((8, 128), 0)
    kx = (lane8 % 64).astype(F32)
    kx2 = kx * kx
    odd8 = (row8 % 2) == 1
    half8 = lane8 < 64

    for k in (1, 2, 3):
        fetches[k].wait()
    noise_half = noise_ref[...]
    noise_full[...] = jnp.concatenate([noise_half, noise_half], axis=0).T
    interp = interp_ref[...]
    for p in range(4):
        cols[p * 128:(p + 1) * 128, :] = jnp.broadcast_to(interp[p:p + 1, :], (128, 128)).T
    lane4 = iota((8, 4), 1)
    focus4 = jnp.broadcast_to(focus_ref[...], (8, 4))
    focus = jnp.sum(jnp.where(lane4 == iota((8, 4), 0) // 2, focus4, 0.0), axis=1, keepdims=True)
    focus = jnp.broadcast_to(focus, (8, 128))
    focus_hi = focus.astype(BF16).astype(F32)
    focus_mid = (focus - focus_hi).astype(BF16).astype(F32)
    weight_in[a, 512:544, :] = jnp.concatenate(
        [focus_hi, focus_mid, focus - focus_hi - focus_mid, jnp.zeros_like(focus)], axis=0
    ).astype(BF16)
    fetches[0].wait()
    wide_p[...] = part_ref[...].astype(F32)

    def weigh(q2, _):
        tiles = []
        for h in range(2):
            q = q2 * 2 + h
            rows = pl.ds(q, 8, stride=64)
            image = wide_p[rows, :]
            ky = jnp.where(odd8, q - 64, q).astype(F32)
            radius = (kx2 + ky * ky) * (1.0 / 16384.0)
            signal = -sine(focus * radius + 0.1) * image
            noise = jnp.where(odd8, noise_full[pl.ds(q + 64, 1), :], noise_full[pl.ds(q, 1), :])
            tiles.append(signal * noise)
            rows_ins[rows, :] = signal * cols[rows, :]
        weight_in[a, pl.ds(pl.multiple_of(q2 * 16, 16), 16), :] = jnp.concatenate(tiles, axis=0).astype(BF16)
        return 0

    def order_proj(q, _):
        tile = wide_x[pl.ds(q, 16, stride=64), :].astype(BF16)
        proj_in[x, pl.ds(pl.multiple_of(q * 16, 16), 16), :] = tile
        return 0

    lax.fori_loop(0, 32, weigh, 0, unroll=4)
    fetches[4].wait()
    wide_x[...] = proj_ref[...].astype(F32)
    lax.fori_loop(0, 64, order_proj, 0, unroll=8)

    fetches[5].wait()
    fetches[6].wait()
    slab, slot = slab_ref[...], slot_ref[...]
    piece = slot // 64
    bucket = (slab * 8 + piece).astype(F32)
    earlier = iota((128, 128), 0) < iota((128, 128), 1)
    ranks = []
    across = [jnp.broadcast_to(bucket[p:p + 1, :], (128, 128)) for p in range(4)]
    down = [b.T for b in across]
    for p in range(4):
        rank = jnp.zeros((1, 128), F32)
        for p2 in range(p + 1):
            same = across[p] == down[p2]
            if p2 == p:
                same = same & earlier
            rank = rank + jnp.sum(jnp.where(same, 1.0, 0.0), axis=0, keepdims=True)
        ranks.append(rank)
    to_plane = (slab // 8) * 4 + piece // 2
    to_column = (piece % 2) * 8 + slab % 8
    base = (to_plane * 64 + to_column * 4).astype(F32)
    position = [base[p:p + 1, :] + ranks[p] for p in range(4)]
    key4 = ((slot % 64) * 4 + iota((4, 128), 0) + 1).astype(F32)
    keys = jnp.concatenate([key4[p:p + 1, :] for p in range(4)], axis=1)
    keys16 = jnp.broadcast_to(keys, (16, 512)).astype(BF16)
    mine16 = iota((16, 128), 0) == u
    ins = rows_ins[...].astype(BF16)
    slot_iota = iota((128, 128), 0).astype(F32)

    def dispatch(chunk, _):
        where = slot_iota + (chunk * 128).astype(F32)
        pick = jnp.concatenate([jnp.where(where == position[p], 1.0, 0.0) for p in range(4)], axis=1).astype(BF16)
        data = dot(pick, ins).astype(BF16)
        tags = dot_nt(keys16, pick)
        for t in range(2):
            meta = tags if t == 0 else pltpu.roll(tags, 64, 1)
            hop1_out[chunk * 2 + t, 0:64, :] = data[t * 64:(t + 1) * 64]
            hop1_out[chunk * 2 + t, 64:80, :] = jnp.where(mine16, meta, 0.0).astype(BF16)
        return 0

    lax.fori_loop(0, 8, dispatch, 0, unroll=2)

    pl.semaphore_wait(barrier, 30)
    each_z(lambda target: w_copy(target, a, target * 2 + core).start())
    t_copy(a).start()
    to_right(0).start()
    to_left(1).start()
    to_right(1).start()
    to_left(0).start()

    def h1_copy(i):
        to = plane(i)
        return copy(hop1_out.at[(u + i) % 16], hop1_in.at[u], h1_send.at[i], h1_recv.at[i], to[0], to[1])

    lax.fori_loop(1, 16, lambda i, _: (h1_copy(i).start(), 0)[1], 0)
    hop1_in[u] = hop1_out[u]

    lane16 = iota((16, 128), 1)
    angle_x = (lane16 % 64).astype(F32) * (2.0 * PI / 128.0)
    cos_x = sine(angle_x + 0.5 * PI)
    sin_x = sine(angle_x) * jnp.where(lane16 < 64, 1.0, -1.0)
    angle_y = iota((64, 128), 0).astype(F32) * (2.0 * PI / 128.0)
    turn_tab[0] = sine(angle_y + 0.5 * PI)
    turn_tab[1] = sine(angle_y) * jnp.where(iota((64, 128), 1) < 64, -1.0, 1.0)
    flip16 = jnp.where(iota((16, 128), 0) % 2 == 1, -1.0, 1.0)

    def views(block):
        row = pl.multiple_of(block * 16, 16)

        def step(k, _):
            for e in range(8):
                q = k * 8 + e
                image_half = proj_in[block, pl.ds(pl.multiple_of(q * 16, 16), 16), :]
                image = image_half.astype(F32)
                lanes = pl.ds(e * 128, 128)
                w = image * (flip16 * turn_tab[0, pl.ds(q, 1), :])
                s = pltpu.roll(image, 64, 1) * (flip16 * turn_tab[1, pl.ds(q, 1), :])
                right_op[k, pl.ds(row, 16), lanes] = (w - s).astype(BF16)
                right_op[k, pl.ds(row + 64, 16), lanes] = image_half
                right_op[k, pl.ds(row + 128, 16), lanes] = (w + s).astype(BF16)
                right_op[k, pl.ds(row + 192, 16), lanes] = (image * image).astype(BF16)
            return 0

        lax.fori_loop(0, 8, step, 0)

    def turns(zz):
        row = pl.multiple_of(zz * 16, 16)
        focus_of = []
        for b in range(2):
            parts = weight_in[zz * 2 + b, 512:544, :].astype(F32)
            focus_of.append(parts[0:8] + parts[8:16] + parts[16:24])

        def step(k, _):
            for e2 in range(4):
                at = pl.ds(pl.multiple_of(k * 64 + e2 * 16, 16), 16)
                first = weight_in[zz * 2, at, :].astype(F32)
                second = weight_in[zz * 2 + 1, at, :].astype(F32)
                for e in range(2):
                    lanes = pl.ds((e2 * 2 + e) * 128, 128)
                    image = jnp.concatenate([first[e * 8:e * 8 + 8], second[e * 8:e * 8 + 8]], axis=0)
                    w = image * cos_x
                    s = pltpu.roll(image, 64, 1) * sin_x
                    left_op[k, pl.ds(row, 16), lanes] = (w - s).astype(BF16)
                    left_op[k, pl.ds(row + 64, 16), lanes] = image.astype(BF16)
                    left_op[k, pl.ds(row + 128, 16), lanes] = (w + s).astype(BF16)
            return 0

        lax.fori_loop(0, 8, step, 0)

        def norms(k, _):
            for e in range(8):
                q = k * 8 + e
                q_hi = q + 32
                ky = (jnp.where(odd8, -64, 0) + jnp.where(half8, q, q_hi)).astype(F32)
                radius = (kx2 + ky * ky) * (1.0 / 16384.0)
                n_lo = jnp.where(odd8, noise_full[pl.ds(q + 64, 1), :], noise_full[pl.ds(q, 1), :])
                n_hi = jnp.where(odd8, noise_full[pl.ds(q_hi + 64, 1), :], noise_full[pl.ds(q_hi, 1), :])
                outs_lo, outs_hi = [], []
                for b in range(2):
                    squared = sine_squared(focus_of[b] * radius + 0.1)
                    turned = pltpu.roll(squared, 64, 1)
                    outs_lo.append(jnp.where(half8, squared, turned) * n_lo)
                    outs_hi.append(jnp.where(half8, turned, squared) * n_hi)
                lanes = pl.ds(e * 128, 128)
                left_op[k, pl.ds(row + 192, 16), lanes] = jnp.concatenate(outs_lo, axis=0).astype(BF16)
                left_op[k + 4, pl.ds(row + 192, 16), lanes] = jnp.concatenate(outs_hi, axis=0).astype(BF16)
            return 0

        lax.fori_loop(0, 4, norms, 0)

    views(x)

    t_copy(a).wait_recv()
    turns(z)
    came_left(0).wait_recv()
    pass_right().start()
    came_right(1).wait_recv()
    pass_left().start()

    @pl.when(relays)
    def _():
        w_copy(relay_from, relay_from * 2 + core, a).wait_recv()
        w_copy(z, relay_from * 2 + core, relay_to * 2 + core).start()
        t_copy(relay_from * 2 + core).start()

    by_distance = (z + 1 - 2 * (z % 2), 2 - z // 2, 3 - 3 * (z // 2))
    for source in by_distance:

        @pl.when(jnp.logical_not(relays & (source == relay_from)))
        def _():
            w_copy(source, source * 2 + core, a).wait_recv()
            t_copy(source * 2 + core).start()

    came_left(1).wait_recv()
    views(from_left)
    came_right(0).wait_recv()
    views(from_right)
    for source in by_distance:
        t_copy(source * 2 + 1 - core).wait_recv()
        turns(source)
    p_copy(4, across_x, 0, right).wait_recv()
    p_copy(5, across_x, 1, left).wait_recv()
    views(across_x)

    part = dot_nt(left_op[0], right_op[0])
    for k in range(1, 8):
        part = part + dot_nt(left_op[k], right_op[k])
    for h in range(2):
        score[h] = part[:, h * 128:(h + 1) * 128]

    m_row, m_col = iota((256, 256), 0), iota((256, 256), 1)
    even = jnp.concatenate([score[h, pl.ds(0, 128, stride=2), :] for h in range(2)], axis=1)
    odd = jnp.concatenate([score[h, pl.ds(1, 128, stride=2), :] for h in range(2)], axis=1)
    folded = even + pltpu.roll(odd, 255, 1)
    lane32 = iota((32, 128), 1)
    penalty = folded[96:128, 128:256]
    penalty = 0.5 * jnp.where(lane32 < 64, pltpu.roll(penalty, 64, 1), penalty)
    penalty = jnp.concatenate([penalty, penalty], axis=1)
    lane = iota((32, 256), 1)
    valid = (lane % 2 == 0) & (lane < 192)
    scores = [jnp.where(valid, folded[s * 32:(s + 1) * 32, :] - penalty, -3e38) for s in range(3)]
    top_score = jnp.max(jnp.maximum(jnp.maximum(scores[0], scores[1]), scores[2]), axis=1, keepdims=True)
    weight = sum(jnp.where(valid, jnp.exp(s - top_score), 0.0) for s in scores)
    same_class = jnp.where((m_row // 2) % 8 == m_col % 8, 1.0, 0.0).astype(BF16)
    own = lane // 8 == iota((32, 256), 0)
    sums = jnp.sum(jnp.where(own, split_dot(weight, same_class), 0.0), axis=0, keepdims=True)
    tops = jnp.sum(jnp.where(own, top_score, 0.0), axis=0, keepdims=True)
    tile = jnp.where(row8 == 0, sums[:, 0:128], 0.0)
    tile = jnp.where(row8 == 1, sums[:, 128:256], tile)
    tile = jnp.where(row8 == 2, tops[:, 0:128], tile)
    stat[v] = jnp.where(row8 == 3, tops[:, 128:256], tile)

    def combine(tiles):
        best = tiles[0]
        for tile in tiles[1:]:
            best = jnp.maximum(best, tile)
        total = jnp.zeros((8, 128), F32)
        for tile in tiles:
            total = total + tile * pltpu.roll(jnp.exp(tile - best), 6, 0)
        return total

    def s_copy(i):
        to = column(i)
        return copy(stat.at[v], stat.at[v], s_send.at[i], s_recv.at[i], to[0], to[1])

    for i in (8, 7, 9, 6, 10, 5, 11, 4, 12, 3, 13, 2, 14, 1, 15):
        s_copy(i).start()

    lax.fori_loop(1, 16, lambda i, _: (h1_copy(i).wait_recv(), 0)[1], 0)
    mix = jnp.where(m_col == ((m_row // 4) % 4) * 64 + (m_row // 16) * 4 + m_row % 4, 1.0, 0.0).astype(BF16)

    def regroup(group, _):
        four = jnp.concatenate([hop1_in[group * 4 + t, 0:64, :] for t in range(4)], axis=0)
        mixed = dot(mix, four).astype(BF16)
        at = pl.ds(pl.multiple_of(group * 16, 16), 16)
        for b in range(16):
            hop2_out[b, at, :] = mixed[b * 16:(b + 1) * 16]
        return 0

    lax.fori_loop(0, 4, regroup, 0)
    meta = hop1_in[0, 64:80, :].astype(F32)
    for t in range(1, 16):
        meta = meta + hop1_in[t, 64:80, :].astype(F32)
    meta = meta.astype(BF16)
    for b in range(16):
        hop2_out[b, 64:80, :] = meta

    def h2_copy(i):
        to = column(i)
        return copy(hop2_out.at[(v + i) % 16], hop2_in.at[v], h2_send.at[i], h2_recv.at[i], to[0], to[1])

    lax.fori_loop(1, 16, lambda i, _: (h2_copy(i).start(), 0)[1], 0)
    hop2_in[v] = hop2_out[v]
    for part in range(2):
        to_right(part).wait_send()
        to_left(part).wait_send()
    pass_right().wait_send()
    pass_left().wait_send()
    each_z(lambda target: w_copy(target, a, target * 2 + core).wait_send())

    @pl.when(relays)
    def _():
        w_copy(z, relay_from * 2 + core, relay_to * 2 + core).wait_send()

    for zz in range(4):
        t_copy(zz * 2 + core).wait_send()
    lax.fori_loop(1, 16, lambda i, _: (h1_copy(i).wait_send(), 0)[1], 0)

    for i in range(1, 16):
        s_copy(i).wait_recv()
    near = combine([stat[i] for i in range(8)])
    far = combine([stat[i] for i in range(8, 16)])
    total = jnp.where(row8 < 2, near, jnp.where(row8 < 4, pltpu.roll(far, 2, 0), 0.0))
    o_row, o_col = iota((128, 128), 0), iota((128, 128), 1)
    same_particle = jnp.where(o_row // 8 == o_col // 8, 1.0, 0.0).astype(BF16)
    class_w = jnp.where(row8 < 4, total / split_dot(total, same_particle), 0.0)
    cw_in[u] = jnp.where(u % 2 == 0, class_w, pltpu.roll(class_w, 4, 0))

    def c_copy(i):
        to = plane(i)
        return copy(cw_in.at[u], cw_in.at[u], c_send.at[i], c_recv.at[i], to[0], to[1])

    for i in (10, 6, 9, 11, 5, 7, 8, 2, 14, 1, 3, 4, 12, 13, 15):
        c_copy(i).start()

    flat = jnp.sum(jnp.where(row8 == z_hi * 2 + z // 2, class_w, 0.0), axis=0, keepdims=True)
    spread = jnp.where(lane8 // 8 == row8 + (z % 2) * 8 + core * 4, flat, 0.0)
    gather_class = jnp.where(o_row % 8 == o_col, 1.0, 0.0).astype(BF16)
    hi = spread.astype(BF16)
    rest = spread - hi.astype(F32)
    cw_flat[...] = dot(hi, gather_class) + split_dot(rest, gather_class)
    cw_ref[...] = cw_flat[0:4, 0:8]

    for i in range(1, 16):
        s_copy(i).wait_send()
    lax.fori_loop(1, 16, lambda i, _: (h2_copy(i).wait_send(), 0)[1], 0)
    lax.fori_loop(1, 16, lambda i, _: (h2_copy(i).wait_recv(), 0)[1], 0)
    pick_key = jnp.where(o_row == v * 4 + o_col % 4, 1.0, 0.0).astype(BF16)
    own_source = lane32 // 4 == iota((32, 128), 0)
    slot64 = iota((64, 128), 0).astype(F32)
    repeats = [jnp.where(o_row == ((o_col % 64) // 4) * 4 + t, 1.0, 0.0).astype(BF16) for t in range(4)]
    vol_ref[...] = jnp.zeros_like(vol_ref)
    lax.fori_loop(1, 16, lambda i, _: (c_copy(i).wait_recv(), 0)[1], 0)

    gathered = [cw_in[2 * m] + cw_in[2 * m + 1] for m in range(8)]
    table = jnp.concatenate(gathered + [jnp.zeros((64, 128), F32)], axis=0).T.astype(BF16)
    for t in range(4):
        coef_tab[t] = dot(table, repeats[t])

    def insert(quad, _):
        parts, rows_in = [], []
        for h in range(2):
            w = quad * 2 + h
            tags = jnp.concatenate([hop2_in[w * 2, 64:80, :], hop2_in[w * 2 + 1, 64:80, :]], axis=0)
            key = jnp.sum(jnp.where(own_source, dot(tags, pick_key), 0.0), axis=0, keepdims=True) - 1.0
            at_slot = jnp.floor(key * 0.25)
            which = key - 4.0 * at_slot
            coef = jnp.zeros((8, 128), F32)
            for p in range(4):
                rows = h * 64 + p * 8
                both = jnp.where(half8, coef_tab[quad, rows:rows + 8, :], coef_tab[quad, rows + 32:rows + 40, :])
                coef = jnp.where(which == float(p), both, coef)
            hit = slot64 == at_slot
            parts.append(
                jnp.concatenate([jnp.where(hit, coef[c:c + 1, :], 0.0) for c in range(8)], axis=0).astype(BF16)
            )
            rows_in += [hop2_in[w * 2, 0:64, :], hop2_in[w * 2 + 1, 0:64, :]]
        vol_ref[...] += dot(jnp.concatenate(parts, axis=1), jnp.concatenate(rows_in, axis=0))
        return 0

    lax.fori_loop(0, 4, insert, 0)
    lax.fori_loop(1, 16, lambda i, _: (c_copy(i).wait_send(), 0)[1], 0)


def per_device(particles, defocus, noise_weight, projections, row_slab, row_slot, interp):
    vmem, dma = pltpu.VMEM, pltpu.SemaphoreType.DMA
    volume, class_weight = pl.pallas_call(
        kernel,
        out_shape=(jax.ShapeDtypeStruct((512, 128), F32), jax.ShapeDtypeStruct((4, 8), F32)),
        in_specs=[pl.BlockSpec(memory_space=pl.ANY)] * 7,
        out_specs=(pl.BlockSpec(memory_space=vmem), pl.BlockSpec(memory_space=vmem)),
        scratch_shapes=[
            vmem((512, 128), BF16),
            vmem((1, 4), F32),
            vmem((64, 128), F32),
            vmem((1024, 128), BF16),
            vmem((4, 128), jnp.int32),
            vmem((4, 128), jnp.int32),
            vmem((4, 128), F32),
            vmem((512, 128), F32),
            vmem((1024, 128), F32),
            vmem((128, 128), F32),
            vmem((512, 128), F32),
            vmem((8, 544, 128), BF16),
            vmem((4, 1024, 128), BF16),
            vmem((512, 128), F32),
            vmem((8, 256, 1024), BF16),
            vmem((8, 256, 1024), BF16),
            vmem((2, 256, 128), F32),
            vmem((2, 64, 128), F32),
            vmem((16, 80, 128), BF16),
            vmem((16, 80, 128), BF16),
            vmem((16, 80, 128), BF16),
            vmem((16, 80, 128), BF16),
            vmem((16, 8, 128), F32),
            vmem((16, 8, 128), F32),
            vmem((8, 128), F32),
            vmem((4, 128, 128), F32),
            dma((7,)), dma((4,)), dma((4,)), dma((4,)), dma((4,)), dma((6,)), dma((6,)), dma((16,)), dma((16,)),
            dma((16,)), dma((16,)), dma((16,)), dma((16,)), dma((16,)), dma((16,)),
        ],
        compiler_params=pltpu.CompilerParams(
            collective_id=0, has_side_effects=True, vmem_limit_bytes=56 * 1024 * 1024
        ),
    )(
        particles.reshape(512, 128), defocus.reshape(1, 4), noise_weight.T, projections.reshape(1024, 128),
        row_slab.reshape(4, 128), row_slot, interp,
    )
    return volume.reshape(8, 64, 128), class_weight


def solution(mesh):
    in_specs = (
        P(("blk", "dom"), None, None),
        P(("blk", "dom")),
        P(),
        P(None, "blk", None, None),
        P(("blk", "dom"), None, None),
        P(("blk", "dom"), None),
        P(("blk", "dom"), None),
    )
    out_specs = (P(None, ("blk", "dom"), None), P(("blk", "dom"), None))
    return jax.shard_map(per_device, mesh=mesh, in_specs=in_specs, out_specs=out_specs, check_vma=False)
```

```python
import jax
import jax.numpy as jnp
from jax import lax
from jax.experimental import pallas as pl
from jax.experimental.pallas import tpu as pltpu
from jax.sharding import PartitionSpec as P

F32, BF16 = jnp.float32, jnp.bfloat16
MESH = pl.DeviceIdType.MESH
FAR = (8, 7, 9, 6, 10, 5, 11, 4, 12, 3, 13, 2, 14, 1, 15)
PI = 3.141592653589793
SIN_COEF = (
    0.9999999992267364, -0.16666665898756483, 0.008333320916259667, -0.00019840515744570079,
    2.7535452887970435e-06, -2.47248903062851e-08, 1.3598699876951359e-10,
)
SIN2_COEF = (
    0.9999999902438815, -0.3333330511544617, 0.044443119935340766, -0.00317232337316227,
    0.00013931019440764148, -3.6240280738953943e-06,
)


def reduced(angle, period, high, mid):
    turns = jnp.floor(angle * (1.0 / period) + 0.5)
    return ((angle - turns * high) - turns * mid) - turns * (period - high - mid)


def horner(coef, y):
    total = jnp.full_like(y, coef[-1])
    for c in coef[-2::-1]:
        total = total * y + c
    return total


def sine(angle):
    r = reduced(angle, 2 * PI, 6.28125, 8117 / 2**22)
    return r * horner(SIN_COEF, r * r)


def sine_squared(angle):
    r = reduced(angle, PI, 3.140625, 8117 / 2**23)
    y = r * r
    return y * horner(SIN2_COEF, y)


def iota(shape, axis):
    return lax.broadcasted_iota(jnp.int32, shape, axis)


def dot(a, b):
    return jnp.dot(a, b, preferred_element_type=F32)


def dot_nt(a, b):
    return lax.dot_general(a, b, (((1,), (1,)), ((), ())), preferred_element_type=F32)


def split_dot(values, indicator):
    high = values.astype(BF16)
    low = (values - high.astype(F32)).astype(BF16)
    return dot(high, indicator) + dot(low, indicator)


def kernel(
    part_hbm, focus_hbm, noise_hbm, proj_hbm, slab_hbm, slot_hbm, interp_hbm,
    vol_ref, cw_ref,
    part_ref, focus_ref, noise_ref, proj_ref, slab_ref, slot_ref, interp_ref,
    wide_p, wide_x, noise_full, cols, weight_in, proj_in, rows_ins,
    left_op, right_op, score, turn_tab, hop1_out, hop1_in, hop2_out, hop2_in,
    stat, cw_in, cw_flat, coef_tab,
    in_sem, w_send, w_recv, t_send, t_recv, p_send, p_recv, h1_send, h1_recv, h2_send, h2_recv,
    s_send, s_recv, c_send, c_recv,
):
    blk, dom = lax.axis_index("blk"), lax.axis_index("dom")
    x, a = blk // 8, blk % 8
    z, core = a // 2, a % 2
    y, z_hi = dom // 2, dom % 2
    u = x * 4 + y
    z_full = z_hi * 4 + z
    v = z_full * 2 + core

    def copy(src, dst, send, recv, to_blk, to_dom):
        return pltpu.make_async_remote_copy(
            src_ref=src, dst_ref=dst, send_sem=send, recv_sem=recv,
            device_id=(to_blk, to_dom), device_id_type=MESH,
        )

    def fetch(k, src, dst):
        return pltpu.make_async_copy(src, dst, in_sem.at[k])

    fetches = [
        fetch(0, part_hbm, part_ref), fetch(1, focus_hbm, focus_ref), fetch(2, noise_hbm, noise_ref),
        fetch(3, interp_hbm, interp_ref), fetch(4, proj_hbm, proj_ref), fetch(5, slab_hbm, slab_ref),
        fetch(6, slot_hbm, slot_ref),
    ]
    for f in fetches:
        f.start()

    other = x * 8 + z * 2 + 1 - core

    def plane(i):
        to = (u + i) % 16
        return (to // 4) * 8 + a, (to % 4) * 2 + z_hi

    def column(i):
        to = (v + i) % 16
        return x * 8 + to % 8, y * 2 + to // 8

    barrier = pltpu.get_barrier_semaphore()

    def greet(who):
        def send(i, _):
            pl.semaphore_signal(barrier, inc=1, device_id=who(i), device_id_type=MESH)
            return 0

        return send

    right, left = ((x + 1) % 4) * 8 + a, ((x + 3) % 4) * 8 + a
    from_left, from_right, across_x = (x + 3) % 4, (x + 1) % 4, (x + 2) % 4
    lax.fori_loop(1, 16, greet(column), 0)
    lax.fori_loop(1, 16, greet(plane), 0)

    def p_copy(k, block, part, to):
        rows = pl.ds(part * 512, 512)
        return copy(proj_in.at[block, rows], proj_in.at[block, rows], p_send.at[k], p_recv.at[k], to, dom)

    def to_right(part):
        return p_copy(part, x, part, right)

    def to_left(part):
        return p_copy(2 + part, x, part, left)

    def came_left(part):
        return p_copy(part, from_left, part, right)

    def came_right(part):
        return p_copy(2 + part, from_right, part, left)

    def pass_right():
        return p_copy(4, from_left, 0, right)

    def pass_left():
        return p_copy(5, from_right, 1, left)

    def w_copy(k, block, to):
        return copy(
            weight_in.at[block], weight_in.at[block], w_send.at[k], w_recv.at[block // 2], x * 8 + to, dom
        )

    def t_copy(block):
        return copy(
            weight_in.at[block], weight_in.at[block], t_send.at[block // 2], t_recv.at[block // 2], other, dom
        )

    def each_z(act):
        for away in (2, 1):
            for sign in (1, -1):
                target = z + sign * away

                @pl.when((target >= 0) & (target < 4))
                def _():
                    act(target)

    relays = (z == 1) | (z == 2)
    relay_from, relay_to = (2 - z) * 3, (z - 1) * 3

    lane8 = iota((8, 128), 1)
    row8 = iota((8, 128), 0)
    kx = (lane8 % 64).astype(F32)
    kx2 = kx * kx
    odd8 = (row8 % 2) == 1
    half8 = lane8 < 64

    for k in (1, 2, 3):
        fetches[k].wait()
    noise_half = noise_ref[...]
    noise_full[...] = jnp.concatenate([noise_half, noise_half], axis=0).T
    interp = interp_ref[...]
    for p in range(4):
        cols[p * 128:(p + 1) * 128, :] = jnp.broadcast_to(interp[p:p + 1, :], (128, 128)).T
    lane4 = iota((8, 4), 1)
    focus4 = jnp.broadcast_to(focus_ref[...], (8, 4))
    focus = jnp.sum(jnp.where(lane4 == iota((8, 4), 0) // 2, focus4, 0.0), axis=1, keepdims=True)
    focus = jnp.broadcast_to(focus, (8, 128))
    focus_hi = focus.astype(BF16).astype(F32)
    focus_mid = (focus - focus_hi).astype(BF16).astype(F32)
    weight_in[a, 512:544, :] = jnp.concatenate(
        [focus_hi, focus_mid, focus - focus_hi - focus_mid, jnp.zeros_like(focus)], axis=0
    ).astype(BF16)
    fetches[0].wait()
    wide_p[...] = part_ref[...].astype(F32)

    def weigh(q2, _):
        tiles = []
        for h in range(2):
            q = q2 * 2 + h
            rows = pl.ds(q, 8, stride=64)
            image = wide_p[rows, :]
            ky = jnp.where(odd8, q - 64, q).astype(F32)
            radius = (kx2 + ky * ky) * (1.0 / 16384.0)
            signal = -sine(focus * radius + 0.1) * image
            noise = jnp.where(odd8, noise_full[pl.ds(q + 64, 1), :], noise_full[pl.ds(q, 1), :])
            tiles.append(signal * noise)
            rows_ins[rows, :] = signal * cols[rows, :]
        weight_in[a, pl.ds(pl.multiple_of(q2 * 16, 16), 16), :] = jnp.concatenate(tiles, axis=0).astype(BF16)
        return 0

    def order_proj(q, _):
        tile = wide_x[pl.ds(q, 16, stride=64), :].astype(BF16)
        proj_in[x, pl.ds(pl.multiple_of(q * 16, 16), 16), :] = tile
        return 0

    lax.fori_loop(0, 32, weigh, 0, unroll=4)
    fetches[4].wait()
    wide_x[...] = proj_ref[...].astype(F32)
    lax.fori_loop(0, 64, order_proj, 0, unroll=8)

    fetches[5].wait()
    fetches[6].wait()
    slab, slot = slab_ref[...], slot_ref[...]
    piece = slot // 64
    bucket = (slab * 8 + piece).astype(F32)
    earlier = iota((128, 128), 0) < iota((128, 128), 1)
    ranks = []
    across = [jnp.broadcast_to(bucket[p:p + 1, :], (128, 128)) for p in range(4)]
    down = [b.T for b in across]
    for p in range(4):
        rank = jnp.zeros((1, 128), F32)
        for p2 in range(p + 1):
            same = across[p] == down[p2]
            if p2 == p:
                same = same & earlier
            rank = rank + jnp.sum(jnp.where(same, 1.0, 0.0), axis=0, keepdims=True)
        ranks.append(rank)
    to_plane = (slab // 8) * 4 + piece // 2
    to_column = (piece % 2) * 8 + slab % 8
    base = (to_plane * 64 + to_column * 4).astype(F32)
    position = [base[p:p + 1, :] + ranks[p] for p in range(4)]
    key4 = ((slot % 64) * 4 + iota((4, 128), 0) + 1).astype(F32)
    keys = jnp.concatenate([key4[p:p + 1, :] for p in range(4)], axis=1)
    keys16 = jnp.broadcast_to(keys, (16, 512)).astype(BF16)
    mine16 = iota((16, 128), 0) == u
    ins = rows_ins[...].astype(BF16)
    slot_iota = iota((128, 128), 0).astype(F32)

    def dispatch(chunk, _):
        where = slot_iota + (chunk * 128).astype(F32)
        pick = jnp.concatenate([jnp.where(where == position[p], 1.0, 0.0) for p in range(4)], axis=1).astype(BF16)
        data = dot(pick, ins).astype(BF16)
        tags = dot_nt(keys16, pick)
        for t in range(2):
            meta = tags if t == 0 else pltpu.roll(tags, 64, 1)
            hop1_out[chunk * 2 + t, 0:64, :] = data[t * 64:(t + 1) * 64]
            hop1_out[chunk * 2 + t, 64:80, :] = jnp.where(mine16, meta, 0.0).astype(BF16)
        return 0

    lax.fori_loop(0, 8, dispatch, 0, unroll=2)

    pl.semaphore_wait(barrier, 30)
    each_z(lambda target: w_copy(target, a, target * 2 + core).start())
    t_copy(a).start()
    to_right(0).start()
    to_left(1).start()
    to_right(1).start()
    to_left(0).start()

    def h1_copy(i):
        to = plane(i)
        return copy(hop1_out.at[(u + i) % 16], hop1_in.at[u], h1_send.at[i], h1_recv.at[i], to[0], to[1])

    lax.fori_loop(1, 16, lambda i, _: (h1_copy(i).start(), 0)[1], 0)
    hop1_in[u] = hop1_out[u]

    lane16 = iota((16, 128), 1)
    angle_x = (lane16 % 64).astype(F32) * (2.0 * PI / 128.0)
    cos_x = sine(angle_x + 0.5 * PI)
    sin_x = sine(angle_x) * jnp.where(lane16 < 64, 1.0, -1.0)
    angle_y = iota((64, 128), 0).astype(F32) * (2.0 * PI / 128.0)
    turn_tab[0] = sine(angle_y + 0.5 * PI)
    turn_tab[1] = sine(angle_y) * jnp.where(iota((64, 128), 1) < 64, -1.0, 1.0)
    flip16 = jnp.where(iota((16, 128), 0) % 2 == 1, -1.0, 1.0)

    def views(block):
        row = pl.multiple_of(block * 16, 16)

        def step(k, _):
            for e in range(8):
                q = k * 8 + e
                image_half = proj_in[block, pl.ds(pl.multiple_of(q * 16, 16), 16), :]
                image = image_half.astype(F32)
                lanes = pl.ds(e * 128, 128)
                w = image * (flip16 * turn_tab[0, pl.ds(q, 1), :])
                s = pltpu.roll(image, 64, 1) * (flip16 * turn_tab[1, pl.ds(q, 1), :])
                right_op[k, pl.ds(row, 16), lanes] = (w - s).astype(BF16)
                right_op[k, pl.ds(row + 64, 16), lanes] = image_half
                right_op[k, pl.ds(row + 128, 16), lanes] = (w + s).astype(BF16)
                right_op[k, pl.ds(row + 192, 16), lanes] = (image * image).astype(BF16)
            return 0

        lax.fori_loop(0, 8, step, 0)

    def turns(zz):
        row = pl.multiple_of(zz * 16, 16)
        focus_of = []
        for b in range(2):
            parts = weight_in[zz * 2 + b, 512:544, :].astype(F32)
            focus_of.append(parts[0:8] + parts[8:16] + parts[16:24])

        def step(k, _):
            for e2 in range(4):
                at = pl.ds(pl.multiple_of(k * 64 + e2 * 16, 16), 16)
                first = weight_in[zz * 2, at, :].astype(F32)
                second = weight_in[zz * 2 + 1, at, :].astype(F32)
                for e in range(2):
                    lanes = pl.ds((e2 * 2 + e) * 128, 128)
                    image = jnp.concatenate([first[e * 8:e * 8 + 8], second[e * 8:e * 8 + 8]], axis=0)
                    w = image * cos_x
                    s = pltpu.roll(image, 64, 1) * sin_x
                    left_op[k, pl.ds(row, 16), lanes] = (w - s).astype(BF16)
                    left_op[k, pl.ds(row + 64, 16), lanes] = image.astype(BF16)
                    left_op[k, pl.ds(row + 128, 16), lanes] = (w + s).astype(BF16)
            return 0

        lax.fori_loop(0, 8, step, 0)

        def norms(k, _):
            for e in range(8):
                q = k * 8 + e
                q_hi = q + 32
                ky = (jnp.where(odd8, -64, 0) + jnp.where(half8, q, q_hi)).astype(F32)
                radius = (kx2 + ky * ky) * (1.0 / 16384.0)
                n_lo = jnp.where(odd8, noise_full[pl.ds(q + 64, 1), :], noise_full[pl.ds(q, 1), :])
                n_hi = jnp.where(odd8, noise_full[pl.ds(q_hi + 64, 1), :], noise_full[pl.ds(q_hi, 1), :])
                outs_lo, outs_hi = [], []
                for b in range(2):
                    squared = sine_squared(focus_of[b] * radius + 0.1)
                    turned = pltpu.roll(squared, 64, 1)
                    outs_lo.append(jnp.where(half8, squared, turned) * n_lo)
                    outs_hi.append(jnp.where(half8, turned, squared) * n_hi)
                lanes = pl.ds(e * 128, 128)
                left_op[k, pl.ds(row + 192, 16), lanes] = jnp.concatenate(outs_lo, axis=0).astype(BF16)
                left_op[k + 4, pl.ds(row + 192, 16), lanes] = jnp.concatenate(outs_hi, axis=0).astype(BF16)
            return 0

        lax.fori_loop(0, 4, norms, 0)

    views(x)

    t_copy(a).wait_recv()
    turns(z)
    m_row, m_col = iota((256, 256), 0), iota((256, 256), 1)
    came_left(0).wait_recv()
    pass_right().start()
    came_right(1).wait_recv()
    pass_left().start()

    @pl.when(relays)
    def _():
        w_copy(relay_from, relay_from * 2 + core, a).wait_recv()
        w_copy(z, relay_from * 2 + core, relay_to * 2 + core).start()
        t_copy(relay_from * 2 + core).start()

    came_left(1).wait_recv()
    views(from_left)

    came_right(0).wait_recv()
    views(from_right)

    by_distance = (z + 1 - 2 * (z % 2), 2 - z // 2, 3 - 3 * (z // 2))
    for source in by_distance:

        @pl.when(jnp.logical_not(relays & (source == relay_from)))
        def _():
            w_copy(source, source * 2 + core, a).wait_recv()
            t_copy(source * 2 + core).start()

    for source in by_distance:
        t_copy(source * 2 + 1 - core).wait_recv()
        turns(source)

    p_copy(4, across_x, 0, right).wait_recv()
    p_copy(5, across_x, 1, left).wait_recv()
    views(across_x)

    part = dot_nt(left_op[0], right_op[0])
    for k in range(1, 8):
        part = part + dot_nt(left_op[k], right_op[k])
    for h in range(2):
        score[h] = part[:, h * 128:(h + 1) * 128]

    even = jnp.concatenate([score[h, pl.ds(0, 128, stride=2), :] for h in range(2)], axis=1)
    odd = jnp.concatenate([score[h, pl.ds(1, 128, stride=2), :] for h in range(2)], axis=1)
    folded = even + pltpu.roll(odd, 255, 1)
    lane32 = iota((32, 128), 1)
    penalty = folded[96:128, 128:256]
    penalty = 0.5 * jnp.where(lane32 < 64, pltpu.roll(penalty, 64, 1), penalty)
    penalty = jnp.concatenate([penalty, penalty], axis=1)
    lane = iota((32, 256), 1)
    valid = (lane % 2 == 0) & (lane < 192)
    scores = [jnp.where(valid, folded[s * 32:(s + 1) * 32, :] - penalty, -3e38) for s in range(3)]
    top_score = jnp.max(jnp.maximum(jnp.maximum(scores[0], scores[1]), scores[2]), axis=1, keepdims=True)
    weight = sum(jnp.where(valid, jnp.exp(s - top_score), 0.0) for s in scores)
    same_class = jnp.where((m_row // 2) % 8 == m_col % 8, 1.0, 0.0).astype(BF16)
    own = lane // 8 == iota((32, 256), 0)
    sums = jnp.sum(jnp.where(own, split_dot(weight, same_class), 0.0), axis=0, keepdims=True)
    tops = jnp.sum(jnp.where(own, top_score, 0.0), axis=0, keepdims=True)
    tile = jnp.where(row8 == 0, sums[:, 0:128], 0.0)
    tile = jnp.where(row8 == 1, sums[:, 128:256], tile)
    tile = jnp.where(row8 == 2, tops[:, 0:128], tile)
    stat[v] = jnp.where(row8 == 3, tops[:, 128:256], tile)

    def combine(tiles):
        best = tiles[0]
        for tile in tiles[1:]:
            best = jnp.maximum(best, tile)
        total = jnp.zeros((8, 128), F32)
        for tile in tiles:
            total = total + tile * pltpu.roll(jnp.exp(tile - best), 6, 0)
        return total

    def s_copy(i):
        to = column(i)
        return copy(stat.at[v], stat.at[v], s_send.at[i], s_recv.at[i], to[0], to[1])

    for i in FAR:
        s_copy(i).start()

    lax.fori_loop(1, 16, lambda i, _: (h1_copy(i).wait_recv(), 0)[1], 0)
    mix = jnp.where(m_col == ((m_row // 4) % 4) * 64 + (m_row // 16) * 4 + m_row % 4, 1.0, 0.0).astype(BF16)

    def regroup(group, _):
        four = jnp.concatenate([hop1_in[group * 4 + t, 0:64, :] for t in range(4)], axis=0)
        mixed = dot(mix, four).astype(BF16)
        at = pl.ds(pl.multiple_of(group * 16, 16), 16)
        for b in range(16):
            hop2_out[b, at, :] = mixed[b * 16:(b + 1) * 16]
        return 0

    lax.fori_loop(0, 4, regroup, 0)
    meta = hop1_in[0, 64:80, :].astype(F32)
    for t in range(1, 16):
        meta = meta + hop1_in[t, 64:80, :].astype(F32)
    meta = meta.astype(BF16)
    for b in range(16):
        hop2_out[b, 64:80, :] = meta

    def h2_copy(i):
        to = column(i)
        return copy(hop2_out.at[(v + i) % 16], hop2_in.at[v], h2_send.at[i], h2_recv.at[i], to[0], to[1])

    for i in FAR:
        h2_copy(i).start()
    hop2_in[v] = hop2_out[v]
    for part in range(2):
        to_right(part).wait_send()
        to_left(part).wait_send()
    pass_right().wait_send()
    pass_left().wait_send()
    each_z(lambda target: w_copy(target, a, target * 2 + core).wait_send())

    @pl.when(relays)
    def _():
        w_copy(z, relay_from * 2 + core, relay_to * 2 + core).wait_send()

    for zz in range(4):
        t_copy(zz * 2 + core).wait_send()
    lax.fori_loop(1, 16, lambda i, _: (h1_copy(i).wait_send(), 0)[1], 0)

    for i in range(1, 16):
        s_copy(i).wait_recv()
    near = combine([stat[i] for i in range(8)])
    far = combine([stat[i] for i in range(8, 16)])
    total = jnp.where(row8 < 2, near, jnp.where(row8 < 4, pltpu.roll(far, 2, 0), 0.0))
    o_row, o_col = iota((128, 128), 0), iota((128, 128), 1)
    same_particle = jnp.where(o_row // 8 == o_col // 8, 1.0, 0.0).astype(BF16)
    class_w = jnp.where(row8 < 4, total / split_dot(total, same_particle), 0.0)
    cw_in[u] = jnp.where(u % 2 == 0, class_w, pltpu.roll(class_w, 4, 0))

    def c_copy(i):
        to = plane(i)
        return copy(cw_in.at[u], cw_in.at[u], c_send.at[i], c_recv.at[i], to[0], to[1])

    for i in (10, 6, 9, 11, 5, 7, 8, 2, 14, 1, 3, 4, 12, 13, 15):
        c_copy(i).start()

    flat = jnp.sum(jnp.where(row8 == z_hi * 2 + z // 2, class_w, 0.0), axis=0, keepdims=True)
    spread = jnp.where(lane8 // 8 == row8 + (z % 2) * 8 + core * 4, flat, 0.0)
    gather_class = jnp.where(o_row % 8 == o_col, 1.0, 0.0).astype(BF16)
    hi = spread.astype(BF16)
    rest = spread - hi.astype(F32)
    cw_flat[...] = dot(hi, gather_class) + split_dot(rest, gather_class)
    cw_ref[...] = cw_flat[0:4, 0:8]

    for i in range(1, 16):
        s_copy(i).wait_send()
    lax.fori_loop(1, 16, lambda i, _: (h2_copy(i).wait_send(), 0)[1], 0)
    lax.fori_loop(1, 16, lambda i, _: (h2_copy(i).wait_recv(), 0)[1], 0)
    pick_key = jnp.where(o_row == v * 4 + o_col % 4, 1.0, 0.0).astype(BF16)
    own_source = lane32 // 4 == iota((32, 128), 0)
    slot64 = iota((64, 128), 0).astype(F32)
    repeats = [jnp.where(o_row == ((o_col % 64) // 4) * 4 + t, 1.0, 0.0).astype(BF16) for t in range(4)]
    slots_of, which_of = [], []
    for w in range(8):
        tags = jnp.concatenate([hop2_in[w * 2, 64:80, :], hop2_in[w * 2 + 1, 64:80, :]], axis=0)
        key = jnp.sum(jnp.where(own_source, dot(tags, pick_key), 0.0), axis=0, keepdims=True) - 1.0
        slots_of.append(jnp.floor(key * 0.25))
        which_of.append(key - 4.0 * slots_of[w])
    lax.fori_loop(1, 16, lambda i, _: (c_copy(i).wait_recv(), 0)[1], 0)

    gathered = [cw_in[2 * m] + cw_in[2 * m + 1] for m in range(8)]
    table = jnp.concatenate(gathered + [jnp.zeros((64, 128), F32)], axis=0).T.astype(BF16)
    for t in range(4):
        coef_tab[t] = dot(table, repeats[t])

    added = jnp.zeros((512, 128), F32)
    for quad in range(4):
        parts, rows_in = [], []
        for h in range(2):
            w = quad * 2 + h
            coef = jnp.zeros((8, 128), F32)
            for p in range(4):
                rows = h * 64 + p * 8
                both = jnp.where(half8, coef_tab[quad, rows:rows + 8, :], coef_tab[quad, rows + 32:rows + 40, :])
                coef = jnp.where(which_of[w] == float(p), both, coef)
            hit = slot64 == slots_of[w]
            parts.append(
                jnp.concatenate([jnp.where(hit, coef[c:c + 1, :], 0.0) for c in range(8)], axis=0).astype(BF16)
            )
            rows_in += [hop2_in[w * 2, 0:64, :], hop2_in[w * 2 + 1, 0:64, :]]
        added = added + dot(jnp.concatenate(parts, axis=1), jnp.concatenate(rows_in, axis=0))
    vol_ref[...] = added
    lax.fori_loop(1, 16, lambda i, _: (c_copy(i).wait_send(), 0)[1], 0)


def per_device(particles, defocus, noise_weight, projections, row_slab, row_slot, interp):
    vmem, dma = pltpu.VMEM, pltpu.SemaphoreType.DMA
    volume, class_weight = pl.pallas_call(
        kernel,
        out_shape=(jax.ShapeDtypeStruct((512, 128), F32), jax.ShapeDtypeStruct((4, 8), F32)),
        in_specs=[pl.BlockSpec(memory_space=pl.ANY)] * 7,
        out_specs=(pl.BlockSpec(memory_space=vmem), pl.BlockSpec(memory_space=vmem)),
        scratch_shapes=[
            vmem((512, 128), BF16),
            vmem((1, 4), F32),
            vmem((64, 128), F32),
            vmem((1024, 128), BF16),
            vmem((4, 128), jnp.int32),
            vmem((4, 128), jnp.int32),
            vmem((4, 128), F32),
            vmem((512, 128), F32),
            vmem((1024, 128), F32),
            vmem((128, 128), F32),
            vmem((512, 128), F32),
            vmem((8, 544, 128), BF16),
            vmem((4, 1024, 128), BF16),
            vmem((512, 128), F32),
            vmem((8, 256, 1024), BF16),
            vmem((8, 256, 1024), BF16),
            vmem((2, 256, 128), F32),
            vmem((2, 64, 128), F32),
            vmem((16, 80, 128), BF16),
            vmem((16, 80, 128), BF16),
            vmem((16, 80, 128), BF16),
            vmem((16, 80, 128), BF16),
            vmem((16, 8, 128), F32),
            vmem((16, 8, 128), F32),
            vmem((8, 128), F32),
            vmem((4, 128, 128), F32),
            dma((7,)), dma((4,)), dma((4,)), dma((4,)), dma((4,)), dma((6,)), dma((6,)), dma((16,)), dma((16,)),
            dma((16,)), dma((16,)), dma((16,)), dma((16,)), dma((16,)), dma((16,)),
        ],
        compiler_params=pltpu.CompilerParams(
            collective_id=0, has_side_effects=True, vmem_limit_bytes=56 * 1024 * 1024
        ),
    )(
        particles.reshape(512, 128), defocus.reshape(1, 4), noise_weight.T, projections.reshape(1024, 128),
        row_slab.reshape(4, 128), row_slot, interp,
    )
    return volume.reshape(8, 64, 128), class_weight


def solution(mesh):
    in_specs = (
        P(("blk", "dom"), None, None),
        P(("blk", "dom")),
        P(),
        P(None, "blk", None, None),
        P(("blk", "dom"), None, None),
        P(("blk", "dom"), None),
        P(("blk", "dom"), None),
    )
    out_specs = (P(None, ("blk", "dom"), None), P(("blk", "dom"), None))
    return jax.shard_map(per_device, mesh=mesh, in_specs=in_specs, out_specs=out_specs, check_vma=False)
```

```python
import jax
import jax.numpy as jnp
from jax import lax
from jax.experimental import pallas as pl
from jax.experimental.pallas import tpu as pltpu
from jax.sharding import PartitionSpec as P

F32, BF16 = jnp.float32, jnp.bfloat16
MESH = pl.DeviceIdType.MESH
FAR = (8, 7, 9, 6, 10, 5, 11, 4, 12, 3, 13, 2, 14, 1, 15)
PI = 3.141592653589793
SIN_COEF = (
    0.9999999992267364, -0.16666665898756483, 0.008333320916259667, -0.00019840515744570079,
    2.7535452887970435e-06, -2.47248903062851e-08, 1.3598699876951359e-10,
)
SIN2_COEF = (
    0.9999999902438815, -0.3333330511544617, 0.044443119935340766, -0.00317232337316227,
    0.00013931019440764148, -3.6240280738953943e-06,
)


def reduced(angle, period, high, mid):
    turns = jnp.floor(angle * (1.0 / period) + 0.5)
    return ((angle - turns * high) - turns * mid) - turns * (period - high - mid)


def horner(coef, y):
    total = jnp.full_like(y, coef[-1])
    for c in coef[-2::-1]:
        total = total * y + c
    return total


def sine(angle):
    r = reduced(angle, 2 * PI, 6.28125, 8117 / 2**22)
    return r * horner(SIN_COEF, r * r)


def sine_squared(angle):
    r = reduced(angle, PI, 3.140625, 8117 / 2**23)
    y = r * r
    return y * horner(SIN2_COEF, y)


def iota(shape, axis):
    return lax.broadcasted_iota(jnp.int32, shape, axis)


def dot(a, b):
    return jnp.dot(a, b, preferred_element_type=F32)


def dot_nt(a, b):
    return lax.dot_general(a, b, (((1,), (1,)), ((), ())), preferred_element_type=F32)


def split_dot(values, indicator):
    high = values.astype(BF16)
    low = (values - high.astype(F32)).astype(BF16)
    return dot(high, indicator) + dot(low, indicator)


def kernel(
    part_hbm, focus_hbm, noise_hbm, proj_hbm, slab_hbm, slot_hbm, interp_hbm,
    vol_ref, cw_ref,
    part_ref, focus_ref, noise_ref, proj_ref, slab_ref, slot_ref, interp_ref,
    wide_p, wide_x, noise_full, cols, weight_in, proj_in, rows_ins,
    left_op, right_op, score, turn_tab, hop1_out, hop1_in, hop2_out, hop2_in,
    stat, cw_in, cw_flat, coef_tab,
    in_sem, w_send, w_recv, t_send, t_recv, p_send, p_recv, h1_send, h1_recv, h2_send, h2_recv,
    s_send, s_recv, c_send, c_recv,
):
    blk, dom = lax.axis_index("blk"), lax.axis_index("dom")
    x, a = blk // 8, blk % 8
    z, core = a // 2, a % 2
    y, z_hi = dom // 2, dom % 2
    u = x * 4 + y
    z_full = z_hi * 4 + z
    v = z_full * 2 + core

    def copy(src, dst, send, recv, to_blk, to_dom):
        return pltpu.make_async_remote_copy(
            src_ref=src, dst_ref=dst, send_sem=send, recv_sem=recv,
            device_id=(to_blk, to_dom), device_id_type=MESH,
        )

    def fetch(k, src, dst):
        return pltpu.make_async_copy(src, dst, in_sem.at[k])

    fetches = [
        fetch(0, part_hbm, part_ref), fetch(1, focus_hbm, focus_ref), fetch(2, noise_hbm, noise_ref),
        fetch(3, interp_hbm, interp_ref), fetch(4, proj_hbm, proj_ref), fetch(5, slab_hbm, slab_ref),
        fetch(6, slot_hbm, slot_ref),
    ]
    for f in fetches:
        f.start()

    other = x * 8 + z * 2 + 1 - core

    def plane(i):
        to = (u + i) % 16
        return (to // 4) * 8 + a, (to % 4) * 2 + z_hi

    def column(i):
        to = (v + i) % 16
        return x * 8 + to % 8, y * 2 + to // 8

    barrier = pltpu.get_barrier_semaphore()

    def greet(who):
        def send(i, _):
            pl.semaphore_signal(barrier, inc=1, device_id=who(i), device_id_type=MESH)
            return 0

        return send

    right, left = ((x + 1) % 4) * 8 + a, ((x + 3) % 4) * 8 + a
    from_left, from_right, across_x = (x + 3) % 4, (x + 1) % 4, (x + 2) % 4
    lax.fori_loop(1, 16, greet(plane), 0)
    lax.fori_loop(1, 16, greet(column), 0)

    def p_copy(k, block, part, to):
        rows = pl.ds(part * 512, 512)
        return copy(proj_in.at[block, rows], proj_in.at[block, rows], p_send.at[k], p_recv.at[k], to, dom)

    def to_right(part):
        return p_copy(part, x, part, right)

    def to_left(part):
        return p_copy(2 + part, x, part, left)

    def came_left(part):
        return p_copy(part, from_left, part, right)

    def came_right(part):
        return p_copy(2 + part, from_right, part, left)

    def pass_right():
        return p_copy(4, from_left, 0, right)

    def pass_left():
        return p_copy(5, from_right, 1, left)

    def w_copy(k, block, to):
        return copy(
            weight_in.at[block], weight_in.at[block], w_send.at[k], w_recv.at[block // 2], x * 8 + to, dom
        )

    def t_copy(block):
        return copy(
            weight_in.at[block], weight_in.at[block], t_send.at[block // 2], t_recv.at[block // 2], other, dom
        )

    def each_z(act):
        for away in (2, 1):
            for sign in (1, -1):
                target = z + sign * away

                @pl.when((target >= 0) & (target < 4))
                def _():
                    act(target)

    relays = (z == 1) | (z == 2)
    relay_from, relay_to = (2 - z) * 3, (z - 1) * 3

    lane8 = iota((8, 128), 1)
    row8 = iota((8, 128), 0)
    kx = (lane8 % 64).astype(F32)
    kx2 = kx * kx
    odd8 = (row8 % 2) == 1
    half8 = lane8 < 64

    for k in (1, 2, 3):
        fetches[k].wait()
    noise_half = noise_ref[...]
    noise_full[...] = jnp.concatenate([noise_half, noise_half], axis=0).T
    interp = interp_ref[...]
    for p in range(4):
        cols[p * 128:(p + 1) * 128, :] = jnp.broadcast_to(interp[p:p + 1, :], (128, 128)).T
    lane4 = iota((8, 4), 1)
    focus4 = jnp.broadcast_to(focus_ref[...], (8, 4))
    focus = jnp.sum(jnp.where(lane4 == iota((8, 4), 0) // 2, focus4, 0.0), axis=1, keepdims=True)
    focus = jnp.broadcast_to(focus, (8, 128))
    focus_hi = focus.astype(BF16).astype(F32)
    focus_mid = (focus - focus_hi).astype(BF16).astype(F32)
    weight_in[a, 512:544, :] = jnp.concatenate(
        [focus_hi, focus_mid, focus - focus_hi - focus_mid, jnp.zeros_like(focus)], axis=0
    ).astype(BF16)
    fetches[0].wait()
    wide_p[...] = part_ref[...].astype(F32)

    def weigh(q2, _):
        tiles = []
        for h in range(2):
            q = q2 * 2 + h
            rows = pl.ds(q, 8, stride=64)
            image = wide_p[rows, :]
            ky = jnp.where(odd8, q - 64, q).astype(F32)
            radius = (kx2 + ky * ky) * (1.0 / 16384.0)
            signal = -sine(focus * radius + 0.1) * image
            noise = jnp.where(odd8, noise_full[pl.ds(q + 64, 1), :], noise_full[pl.ds(q, 1), :])
            tiles.append(signal * noise)
            rows_ins[rows, :] = signal * cols[rows, :]
        weight_in[a, pl.ds(pl.multiple_of(q2 * 16, 16), 16), :] = jnp.concatenate(tiles, axis=0).astype(BF16)
        return 0

    def order_proj(q, _):
        tile = wide_x[pl.ds(q, 16, stride=64), :].astype(BF16)
        proj_in[x, pl.ds(pl.multiple_of(q * 16, 16), 16), :] = tile
        return 0

    lax.fori_loop(0, 32, weigh, 0, unroll=4)
    fetches[4].wait()
    wide_x[...] = proj_ref[...].astype(F32)
    lax.fori_loop(0, 64, order_proj, 0, unroll=8)

    pl.semaphore_wait(barrier, 30)
    each_z(lambda target: w_copy(target, a, target * 2 + core).start())
    t_copy(a).start()
    to_right(0).start()
    to_left(1).start()
    to_right(1).start()
    to_left(0).start()

    fetches[5].wait()
    fetches[6].wait()
    slab, slot = slab_ref[...], slot_ref[...]
    piece = slot // 64
    bucket = (slab * 8 + piece).astype(F32)
    earlier = iota((128, 128), 0) < iota((128, 128), 1)
    ranks = []
    across = [jnp.broadcast_to(bucket[p:p + 1, :], (128, 128)) for p in range(4)]
    down = [b.T for b in across]
    for p in range(4):
        rank = jnp.zeros((1, 128), F32)
        for p2 in range(p + 1):
            same = across[p] == down[p2]
            if p2 == p:
                same = same & earlier
            rank = rank + jnp.sum(jnp.where(same, 1.0, 0.0), axis=0, keepdims=True)
        ranks.append(rank)
    to_plane = (slab // 8) * 4 + piece // 2
    to_column = (piece % 2) * 8 + slab % 8
    base = (to_plane * 64 + to_column * 4).astype(F32)
    position = [base[p:p + 1, :] + ranks[p] for p in range(4)]
    key4 = ((slot % 64) * 4 + iota((4, 128), 0) + 1).astype(F32)
    keys = jnp.concatenate([key4[p:p + 1, :] for p in range(4)], axis=1)
    keys16 = jnp.broadcast_to(keys, (16, 512)).astype(BF16)
    mine16 = iota((16, 128), 0) == u
    ins = rows_ins[...].astype(BF16)
    slot_iota = iota((128, 128), 0).astype(F32)

    def dispatch(chunk, _):
        where = slot_iota + (chunk * 128).astype(F32)
        pick = jnp.concatenate([jnp.where(where == position[p], 1.0, 0.0) for p in range(4)], axis=1).astype(BF16)
        data = dot(pick, ins).astype(BF16)
        tags = dot_nt(keys16, pick)
        for t in range(2):
            meta = tags if t == 0 else pltpu.roll(tags, 64, 1)
            hop1_out[chunk * 2 + t, 0:64, :] = data[t * 64:(t + 1) * 64]
            hop1_out[chunk * 2 + t, 64:80, :] = jnp.where(mine16, meta, 0.0).astype(BF16)
        return 0

    lax.fori_loop(0, 8, dispatch, 0, unroll=2)

    def h1_copy(i):
        to = plane(i)
        return copy(hop1_out.at[(u + i) % 16], hop1_in.at[u], h1_send.at[i], h1_recv.at[i], to[0], to[1])

    lax.fori_loop(1, 16, lambda i, _: (h1_copy(i).start(), 0)[1], 0)
    hop1_in[u] = hop1_out[u]

    lane16 = iota((16, 128), 1)
    angle_x = (lane16 % 64).astype(F32) * (2.0 * PI / 128.0)
    cos_x = sine(angle_x + 0.5 * PI)
    sin_x = sine(angle_x) * jnp.where(lane16 < 64, 1.0, -1.0)
    angle_y = iota((64, 128), 0).astype(F32) * (2.0 * PI / 128.0)
    turn_tab[0] = sine(angle_y + 0.5 * PI)
    turn_tab[1] = sine(angle_y) * jnp.where(iota((64, 128), 1) < 64, -1.0, 1.0)
    flip16 = jnp.where(iota((16, 128), 0) % 2 == 1, -1.0, 1.0)

    def views(block):
        row = pl.multiple_of(block * 16, 16)

        def step(k, _):
            for e in range(8):
                q = k * 8 + e
                image_half = proj_in[block, pl.ds(pl.multiple_of(q * 16, 16), 16), :]
                image = image_half.astype(F32)
                lanes = pl.ds(e * 128, 128)
                w = image * (flip16 * turn_tab[0, pl.ds(q, 1), :])
                s = pltpu.roll(image, 64, 1) * (flip16 * turn_tab[1, pl.ds(q, 1), :])
                right_op[k, pl.ds(row, 16), lanes] = (w - s).astype(BF16)
                right_op[k, pl.ds(row + 64, 16), lanes] = image_half
                right_op[k, pl.ds(row + 128, 16), lanes] = (w + s).astype(BF16)
                right_op[k, pl.ds(row + 192, 16), lanes] = (image * image).astype(BF16)
            return 0

        lax.fori_loop(0, 8, step, 0)

    def turns(zz):
        row = pl.multiple_of(zz * 16, 16)
        focus_of = []
        for b in range(2):
            parts = weight_in[zz * 2 + b, 512:544, :].astype(F32)
            focus_of.append(parts[0:8] + parts[8:16] + parts[16:24])

        def step(k, _):
            for e2 in range(4):
                at = pl.ds(pl.multiple_of(k * 64 + e2 * 16, 16), 16)
                first = weight_in[zz * 2, at, :].astype(F32)
                second = weight_in[zz * 2 + 1, at, :].astype(F32)
                for e in range(2):
                    lanes = pl.ds((e2 * 2 + e) * 128, 128)
                    image = jnp.concatenate([first[e * 8:e * 8 + 8], second[e * 8:e * 8 + 8]], axis=0)
                    w = image * cos_x
                    s = pltpu.roll(image, 64, 1) * sin_x
                    left_op[k, pl.ds(row, 16), lanes] = (w - s).astype(BF16)
                    left_op[k, pl.ds(row + 64, 16), lanes] = image.astype(BF16)
                    left_op[k, pl.ds(row + 128, 16), lanes] = (w + s).astype(BF16)
            return 0

        lax.fori_loop(0, 8, step, 0)

        def norms(k, _):
            for e in range(8):
                q = k * 8 + e
                q_hi = q + 32
                ky = (jnp.where(odd8, -64, 0) + jnp.where(half8, q, q_hi)).astype(F32)
                radius = (kx2 + ky * ky) * (1.0 / 16384.0)
                n_lo = jnp.where(odd8, noise_full[pl.ds(q + 64, 1), :], noise_full[pl.ds(q, 1), :])
                n_hi = jnp.where(odd8, noise_full[pl.ds(q_hi + 64, 1), :], noise_full[pl.ds(q_hi, 1), :])
                outs_lo, outs_hi = [], []
                for b in range(2):
                    squared = sine_squared(focus_of[b] * radius + 0.1)
                    turned = pltpu.roll(squared, 64, 1)
                    outs_lo.append(jnp.where(half8, squared, turned) * n_lo)
                    outs_hi.append(jnp.where(half8, turned, squared) * n_hi)
                lanes = pl.ds(e * 128, 128)
                left_op[k, pl.ds(row + 192, 16), lanes] = jnp.concatenate(outs_lo, axis=0).astype(BF16)
                left_op[k + 4, pl.ds(row + 192, 16), lanes] = jnp.concatenate(outs_hi, axis=0).astype(BF16)
            return 0

        lax.fori_loop(0, 4, norms, 0)

    views(x)

    t_copy(a).wait_recv()
    turns(z)
    m_row, m_col = iota((256, 256), 0), iota((256, 256), 1)
    came_left(0).wait_recv()
    pass_right().start()
    came_right(1).wait_recv()
    pass_left().start()

    @pl.when(relays)
    def _():
        w_copy(relay_from, relay_from * 2 + core, a).wait_recv()
        w_copy(z, relay_from * 2 + core, relay_to * 2 + core).start()
        t_copy(relay_from * 2 + core).start()

    came_left(1).wait_recv()
    views(from_left)

    came_right(0).wait_recv()
    views(from_right)

    by_distance = (z + 1 - 2 * (z % 2), 2 - z // 2, 3 - 3 * (z // 2))
    for source in by_distance:

        @pl.when(jnp.logical_not(relays & (source == relay_from)))
        def _():
            w_copy(source, source * 2 + core, a).wait_recv()
            t_copy(source * 2 + core).start()

    for source in by_distance:
        t_copy(source * 2 + 1 - core).wait_recv()
        turns(source)

    p_copy(4, across_x, 0, right).wait_recv()
    p_copy(5, across_x, 1, left).wait_recv()
    views(across_x)

    part = dot_nt(left_op[0], right_op[0])
    for k in range(1, 8):
        part = part + dot_nt(left_op[k], right_op[k])
    for h in range(2):
        score[h] = part[:, h * 128:(h + 1) * 128]

    even = jnp.concatenate([score[h, pl.ds(0, 128, stride=2), :] for h in range(2)], axis=1)
    odd = jnp.concatenate([score[h, pl.ds(1, 128, stride=2), :] for h in range(2)], axis=1)
    folded = even + pltpu.roll(odd, 255, 1)
    lane32 = iota((32, 128), 1)
    penalty = folded[96:128, 128:256]
    penalty = 0.5 * jnp.where(lane32 < 64, pltpu.roll(penalty, 64, 1), penalty)
    penalty = jnp.concatenate([penalty, penalty], axis=1)
    lane = iota((32, 256), 1)
    valid = (lane % 2 == 0) & (lane < 192)
    scores = [jnp.where(valid, folded[s * 32:(s + 1) * 32, :] - penalty, -3e38) for s in range(3)]
    top_score = jnp.max(jnp.maximum(jnp.maximum(scores[0], scores[1]), scores[2]), axis=1, keepdims=True)
    weight = sum(jnp.where(valid, jnp.exp(s - top_score), 0.0) for s in scores)
    same_class = jnp.where((m_row // 2) % 8 == m_col % 8, 1.0, 0.0).astype(BF16)
    own = lane // 8 == iota((32, 256), 0)
    sums = jnp.sum(jnp.where(own, split_dot(weight, same_class), 0.0), axis=0, keepdims=True)
    tops = jnp.sum(jnp.where(own, top_score, 0.0), axis=0, keepdims=True)
    tile = jnp.where(row8 == 0, sums[:, 0:128], 0.0)
    tile = jnp.where(row8 == 1, sums[:, 128:256], tile)
    tile = jnp.where(row8 == 2, tops[:, 0:128], tile)
    stat[v] = jnp.where(row8 == 3, tops[:, 128:256], tile)

    def combine(tiles):
        best = tiles[0]
        for tile in tiles[1:]:
            best = jnp.maximum(best, tile)
        total = jnp.zeros((8, 128), F32)
        for tile in tiles:
            total = total + tile * pltpu.roll(jnp.exp(tile - best), 6, 0)
        return total

    def s_copy(i):
        to = column(i)
        return copy(stat.at[v], stat.at[v], s_send.at[i], s_recv.at[i], to[0], to[1])

    for i in FAR:
        s_copy(i).start()

    lax.fori_loop(1, 16, lambda i, _: (h1_copy(i).wait_recv(), 0)[1], 0)
    mix = jnp.where(m_col == ((m_row // 4) % 4) * 64 + (m_row // 16) * 4 + m_row % 4, 1.0, 0.0).astype(BF16)

    def regroup(group, _):
        four = jnp.concatenate([hop1_in[group * 4 + t, 0:64, :] for t in range(4)], axis=0)
        mixed = dot(mix, four).astype(BF16)
        at = pl.ds(pl.multiple_of(group * 16, 16), 16)
        for b in range(16):
            hop2_out[b, at, :] = mixed[b * 16:(b + 1) * 16]
        return 0

    lax.fori_loop(0, 4, regroup, 0)
    meta = hop1_in[0, 64:80, :].astype(F32)
    for t in range(1, 16):
        meta = meta + hop1_in[t, 64:80, :].astype(F32)
    meta = meta.astype(BF16)
    for b in range(16):
        hop2_out[b, 64:80, :] = meta

    def h2_copy(i):
        to = column(i)
        return copy(hop2_out.at[(v + i) % 16], hop2_in.at[v], h2_send.at[i], h2_recv.at[i], to[0], to[1])

    for i in FAR:
        h2_copy(i).start()
    hop2_in[v] = hop2_out[v]
    for part in range(2):
        to_right(part).wait_send()
        to_left(part).wait_send()
    pass_right().wait_send()
    pass_left().wait_send()
    each_z(lambda target: w_copy(target, a, target * 2 + core).wait_send())

    @pl.when(relays)
    def _():
        w_copy(z, relay_from * 2 + core, relay_to * 2 + core).wait_send()

    for zz in range(4):
        t_copy(zz * 2 + core).wait_send()
    lax.fori_loop(1, 16, lambda i, _: (h1_copy(i).wait_send(), 0)[1], 0)

    for i in range(1, 16):
        s_copy(i).wait_recv()
    near = combine([stat[i] for i in range(8)])
    far = combine([stat[i] for i in range(8, 16)])
    total = jnp.where(row8 < 2, near, jnp.where(row8 < 4, pltpu.roll(far, 2, 0), 0.0))
    o_row, o_col = iota((128, 128), 0), iota((128, 128), 1)
    same_particle = jnp.where(o_row // 8 == o_col // 8, 1.0, 0.0).astype(BF16)
    class_w = jnp.where(row8 < 4, total / split_dot(total, same_particle), 0.0)
    cw_in[u] = jnp.where(u % 2 == 0, class_w, pltpu.roll(class_w, 4, 0))

    def c_copy(i):
        to = plane(i)
        return copy(cw_in.at[u], cw_in.at[u], c_send.at[i], c_recv.at[i], to[0], to[1])

    for i in (10, 6, 9, 11, 5, 7, 8, 2, 14, 1, 3, 4, 12, 13, 15):
        c_copy(i).start()

    flat = jnp.sum(jnp.where(row8 == z_hi * 2 + z // 2, class_w, 0.0), axis=0, keepdims=True)
    spread = jnp.where(lane8 // 8 == row8 + (z % 2) * 8 + core * 4, flat, 0.0)
    gather_class = jnp.where(o_row % 8 == o_col, 1.0, 0.0).astype(BF16)
    hi = spread.astype(BF16)
    rest = spread - hi.astype(F32)
    cw_flat[...] = dot(hi, gather_class) + split_dot(rest, gather_class)
    cw_ref[...] = cw_flat[0:4, 0:8]

    for i in range(1, 16):
        s_copy(i).wait_send()
    lax.fori_loop(1, 16, lambda i, _: (h2_copy(i).wait_send(), 0)[1], 0)
    lax.fori_loop(1, 16, lambda i, _: (h2_copy(i).wait_recv(), 0)[1], 0)
    pick_key = jnp.where(o_row == v * 4 + o_col % 4, 1.0, 0.0).astype(BF16)
    own_source = lane32 // 4 == iota((32, 128), 0)
    slot64 = iota((64, 128), 0).astype(F32)
    repeats = [jnp.where(o_row == ((o_col % 64) // 4) * 4 + t, 1.0, 0.0).astype(BF16) for t in range(4)]
    slots_of, which_of = [], []
    for w in range(8):
        tags = jnp.concatenate([hop2_in[w * 2, 64:80, :], hop2_in[w * 2 + 1, 64:80, :]], axis=0)
        key = jnp.sum(jnp.where(own_source, dot(tags, pick_key), 0.0), axis=0, keepdims=True) - 1.0
        slots_of.append(jnp.floor(key * 0.25))
        which_of.append(key - 4.0 * slots_of[w])
    lax.fori_loop(1, 16, lambda i, _: (c_copy(i).wait_recv(), 0)[1], 0)

    gathered = [cw_in[2 * m] + cw_in[2 * m + 1] for m in range(8)]
    table = jnp.concatenate(gathered + [jnp.zeros((64, 128), F32)], axis=0).T.astype(BF16)
    for t in range(4):
        coef_tab[t] = dot(table, repeats[t])

    added = jnp.zeros((512, 128), F32)
    for quad in range(4):
        parts, rows_in = [], []
        for h in range(2):
            w = quad * 2 + h
            coef = jnp.zeros((8, 128), F32)
            for p in range(4):
                rows = h * 64 + p * 8
                both = jnp.where(half8, coef_tab[quad, rows:rows + 8, :], coef_tab[quad, rows + 32:rows + 40, :])
                coef = jnp.where(which_of[w] == float(p), both, coef)
            hit = slot64 == slots_of[w]
            parts.append(
                jnp.concatenate([jnp.where(hit, coef[c:c + 1, :], 0.0) for c in range(8)], axis=0).astype(BF16)
            )
            rows_in += [hop2_in[w * 2, 0:64, :], hop2_in[w * 2 + 1, 0:64, :]]
        added = added + dot(jnp.concatenate(parts, axis=1), jnp.concatenate(rows_in, axis=0))
    vol_ref[...] = added
    lax.fori_loop(1, 16, lambda i, _: (c_copy(i).wait_send(), 0)[1], 0)


def per_device(particles, defocus, noise_weight, projections, row_slab, row_slot, interp):
    vmem, dma = pltpu.VMEM, pltpu.SemaphoreType.DMA
    volume, class_weight = pl.pallas_call(
        kernel,
        out_shape=(jax.ShapeDtypeStruct((512, 128), F32), jax.ShapeDtypeStruct((4, 8), F32)),
        in_specs=[pl.BlockSpec(memory_space=pl.ANY)] * 7,
        out_specs=(pl.BlockSpec(memory_space=vmem), pl.BlockSpec(memory_space=vmem)),
        scratch_shapes=[
            vmem((512, 128), BF16),
            vmem((1, 4), F32),
            vmem((64, 128), F32),
            vmem((1024, 128), BF16),
            vmem((4, 128), jnp.int32),
            vmem((4, 128), jnp.int32),
            vmem((4, 128), F32),
            vmem((512, 128), F32),
            vmem((1024, 128), F32),
            vmem((128, 128), F32),
            vmem((512, 128), F32),
            vmem((8, 544, 128), BF16),
            vmem((4, 1024, 128), BF16),
            vmem((512, 128), F32),
            vmem((8, 256, 1024), BF16),
            vmem((8, 256, 1024), BF16),
            vmem((2, 256, 128), F32),
            vmem((2, 64, 128), F32),
            vmem((16, 80, 128), BF16),
            vmem((16, 80, 128), BF16),
            vmem((16, 80, 128), BF16),
            vmem((16, 80, 128), BF16),
            vmem((16, 8, 128), F32),
            vmem((16, 8, 128), F32),
            vmem((8, 128), F32),
            vmem((4, 128, 128), F32),
            dma((7,)), dma((4,)), dma((4,)), dma((4,)), dma((4,)), dma((6,)), dma((6,)), dma((16,)), dma((16,)),
            dma((16,)), dma((16,)), dma((16,)), dma((16,)), dma((16,)), dma((16,)),
        ],
        compiler_params=pltpu.CompilerParams(
            collective_id=0, has_side_effects=True, vmem_limit_bytes=56 * 1024 * 1024
        ),
    )(
        particles.reshape(512, 128), defocus.reshape(1, 4), noise_weight.T, projections.reshape(1024, 128),
        row_slab.reshape(4, 128), row_slot, interp,
    )
    return volume.reshape(8, 64, 128), class_weight


def solution(mesh):
    in_specs = (
        P(("blk", "dom"), None, None),
        P(("blk", "dom")),
        P(),
        P(None, "blk", None, None),
        P(("blk", "dom"), None, None),
        P(("blk", "dom"), None),
        P(("blk", "dom"), None),
    )
    out_specs = (P(None, ("blk", "dom"), None), P(("blk", "dom"), None))
    return jax.shard_map(per_device, mesh=mesh, in_specs=in_specs, out_specs=out_specs, check_vma=False)
```
